256 devices in a mesh: wire: 128 (over x, z_hi, y, core), col: 2 (over z_lo).
Axes of the slice: x: 4, y: 4, z: 8 (z_hi: 4, z_lo: 2; z = z_hi * 2 + z_lo), core: 2. Of those that a mesh axis runs over, the one named last changes fastest.
Arguments:
- hamiltonian: bfloat16 [2048, 3, 128, 128], P('wire')
- offsets: int32 [2048, 3], P('wire'), may hold values from -2 to 2, as said below
- phase_left: bfloat16 [262144, 2048], P('wire'), may hold values from -0.125 to 0.125
- phase_right: bfloat16 [262144, 2048], P('wire'), may hold values from -0.01171875 to 0.01171875
- orbitals: bfloat16 [262144, 512], P('wire', 'col'), may hold values from -6 to 6
Outputs:
- gradient: float32 [262144, 512], P('wire', 'col')
The draws below stay inside these ranges and needn't reach their ends.
Inputs may be any that keep to these rules, and one draw needn't show every extreme that they name: `offsets`: slot 0 of every row block has offset 0.
All inputs are finite; a program needn't handle non-finite values.
Results may differ from the reference program's by a relative error of at most 0.0017.
Values may be sent and summed in bfloat16 or wider, within the bound.
A program may use at most 128 MiB of HBM per device.

```python
import jax
import jax.numpy as jnp
from jax import lax

B = 128
REACH = 2
SLOTS = 3
M = 512
K = 2048
NBLK = 2048
ROWS = 262144


def draw_hamiltonian(key, part):
    noise_key = jax.random.fold_in(key, 11)
    site_key = jax.random.fold_in(key, 12)
    noise = jax.random.normal(noise_key, (NBLK, SLOTS, B, B), jnp.float32)
    noise = noise * (SLOTS * B) ** (-0.5)
    onsite = jax.random.uniform(site_key, (NBLK, B), jnp.float32, 0.5, 3.5)
    eye = jnp.eye(B, dtype=jnp.float32)
    first = noise[:, 0] + onsite[:, :, None] * eye[None]
    return jnp.concatenate([first[:, None], noise[:, 1:]], axis=1).astype(jnp.bfloat16)


def draw_offsets(key, part):
    drawn = jax.random.randint(jax.random.fold_in(key, 21), (NBLK, SLOTS - 1), 0 - REACH, REACH + 1, dtype=jnp.int32)
    drawn = drawn.at[0, 0].set(REACH).at[0, SLOTS - 2].set(0 - REACH)
    return jnp.concatenate([jnp.zeros((NBLK, 1), jnp.int32), drawn], axis=1)


def steps_of(key, dims, split, least, largest):
    factor_of = 1.0
    for position, shards_of in split:
        heights = jax.random.uniform(jax.random.fold_in(jax.random.fold_in(key, 6), position), (shards_of,), jnp.float32, least / len(split), largest / len(split))
        factor_of = factor_of * jnp.repeat(jnp.exp(heights), dims[position] // shards_of).reshape((-1,) + (1,) * (len(dims) - 1 - position))
    return factor_of


def normal_values(stream_key, dims, scale, reach, split=(), held_as=jnp.bfloat16):
    values = jax.random.normal(stream_key, dims, jnp.float32) * scale
    if len(split) > 0:
        values = steps_of(stream_key, dims, split, -0.22, 0.18) * values
    return jnp.clip(values, min=-reach, max=reach).astype(held_as)


def setup_inputs(seed: int = 0) -> dict:
    key_list = jax.random.split(jax.random.key(seed), 6)
    return {
        "hamiltonian": draw_hamiltonian(jax.random.fold_in(key_list[5], 71), 0),
        "offsets": draw_offsets(jax.random.fold_in(key_list[5], 71), 0),
        "phase_left": normal_values(key_list[2], (ROWS, K), K ** -0.5, 0.125, ((0, 128),)),
        "phase_right": normal_values(key_list[3], (ROWS, K), ROWS ** -0.5, 0.01171875, ((0, 128),)),
        "orbitals": normal_values(key_list[4], (ROWS, M), 1.0, 6.0, ((0, 128), (1, 2))),
    }


def band_product(hamiltonian, offsets, orbitals):
    tiles = orbitals.reshape(NBLK, B, M).astype(jnp.float32)

    def one_block(packed):
        block_index, weights, shifts = packed
        picked = jnp.take(tiles, (block_index + shifts) % NBLK, axis=0)
        return jnp.einsum('sab,sbm->am', weights.astype(jnp.float32), picked)

    result = lax.map(one_block, (jnp.arange(NBLK, dtype=jnp.int32), hamiltonian, offsets))
    return result.reshape(ROWS, M)


def reference(hamiltonian, offsets, phase_left, phase_right, orbitals):
    band = band_product(hamiltonian, offsets, orbitals)
    coupling = jnp.dot(phase_right.T, orbitals, preferred_element_type=jnp.float32).astype(jnp.bfloat16)
    image = band + jnp.dot(phase_left, coupling, preferred_element_type=jnp.float32)
    wide = orbitals.astype(jnp.float32)
    intersection = jnp.dot(orbitals.T, orbitals, preferred_element_type=jnp.float32) / ROWS
    cross = jnp.dot(wide.T, image, precision=lax.Precision.HIGHEST) / ROWS
    gradient = 2.0 * image - jnp.dot(image, intersection, precision=lax.Precision.HIGHEST) - jnp.dot(wide, cross, precision=lax.Precision.HIGHEST)
    return gradient
```

```python
import jax
import jax.numpy as jnp
from jax import lax
from jax.experimental import pallas as pl
from jax.experimental.pallas import tpu as pltpu
from jax.sharding import Mesh
from jax.sharding import PartitionSpec as P

F32, BF16 = jnp.float32, jnp.bfloat16
MESH = pl.DeviceIdType.MESH
AXES = ("x", "zh", "y", "core", "zl")
WIRE = ("x", "zh", "y", "core")
SIDE, ZHI, ZALL = 4, 4, 8
LANES = 2
HALO, ROWS, COLS, KDIM, BLK = 256, 2048, 256, 2048, 128
HALF = KDIM // 2
TOTAL = 262144
TILE = 256


def mm(a, b):
    return jnp.dot(a, b, preferred_element_type=F32)


def mm_nt(a, b):
    return lax.dot_general(a, b, (((1,), (1,)), ((), ())), preferred_element_type=F32)


def split(v):
    hi = v.astype(BF16)
    return hi, (v - hi.astype(F32)).astype(BF16)


def at(start, size):
    return pl.ds(pl.multiple_of(start, size), size)


def near(src, i):
    return [src[at((i + r) * BLK, BLK), :] for r in range(5)]


def pick(blocks, shift):
    chosen = blocks[2]
    for r in (0, 1, 3, 4):
        chosen = jnp.where(shift == r - 2, blocks[r], chosen)
    return chosen


class Links:
    def __init__(self, send_sems, recv_sems):
        self.send_sems, self.recv_sems, self.started = send_sems, recv_sems, []

    def send(self, src, dst, **where):
        i = len(self.started)
        copy = pltpu.make_async_remote_copy(
            src_ref=src,
            dst_ref=dst,
            send_sem=self.send_sems.at[i],
            recv_sem=self.recv_sems.at[i],
            device_id=where,
            device_id_type=MESH,
        )
        copy.start()
        self.started.append(copy)
        return copy

    def finish(self):
        for copy in self.started:
            copy.wait_send()


N_SEMS = 160


def kernel(
    ham, off, phase_l, phase_r, orb, out,
    o_m, o_o, ot_m, ot_o, pr, plv, hv,
    core_tx, core_rx, acc, rx1, s1, rx2, s2, rx3, ct, band,
    s_q, s_crx, s_acc, s_rx1, s_s1, s_rx2, s_z, s_res,
    c_q, c_crx, c_acc, c_rx1, c_s1, c_rx2, c_z, c_res,
    d_hi, d_lo, y_hi, y_lo,
    load_sems, send_sems, recv_sems,
):
    at_axis = {a: lax.axis_index(a) for a in AXES}
    core, zl, zh = at_axis["core"], at_axis["zl"], at_axis["zh"]
    other = 1 - core
    z = zh * 2 + zl
    wire = ((at_axis["x"] * ZHI + zh) * SIDE + at_axis["y"]) * 2 + core
    n_wire = 128

    def step(axis, d):
        return {axis: lax.rem(at_axis[axis] + d, SIDE)}

    def along_z(d):
        there = lax.rem(z + d, ZALL)
        return {"zh": there // 2, "zl": lax.rem(there, 2)}

    def on_wire(d):
        w = lax.rem(wire + d + n_wire, n_wire)
        return {
            "x": w // (ZHI * SIDE * 2),
            "zh": lax.rem(w // (SIDE * 2), ZHI),
            "y": lax.rem(w // 2, SIDE),
            "core": lax.rem(w, 2),
        }

    links = Links(send_sems, recv_sems)
    own = pl.ds(HALO, ROWS)

    def load(src, dst, i):
        copy = pltpu.make_async_copy(src, dst, load_sems.at[i])
        copy.start()
        return copy

    get_o = load(orb, o_m.at[own, :], 0)
    get_pr = []
    for i in range(4):
        start = (other if i < 2 else core) * HALF + (i % 2) * 512
        cols = at(start, 512)
        get_pr.append(load(phase_r.at[:, cols], pr.at[:, cols], 1 + i))
    get_h = load(ham, hv, 5)
    get_pl = load(phase_l, plv, 6)

    barrier = pltpu.get_barrier_semaphore()
    greeted = [step(a, d) for a in ("x", "y") for d in (1, 2, 3)]
    greeted += [along_z(d) for d in range(1, ZALL)]
    greeted += [{"core": other}, on_wire(1), on_wire(-1)]
    for where in greeted:
        pl.semaphore_signal(barrier, inc=1, device_id=where, device_id_type=MESH)

    get_o.wait()

    def turn(src, dst):
        @pl.loop(0, ROWS // TILE)
        def _(t):
            dst[:, at(t * TILE, TILE)] = src[pl.ds(pl.multiple_of(HALO + t * TILE, TILE), TILE), :].T

    turn(o_m, ot_m)
    pl.semaphore_wait(barrier, len(greeted))

    swap = links.send(o_m.at[own, :], o_o.at[own, :], zl=1 - zl)
    last, first = pl.ds(ROWS, HALO), pl.ds(HALO, HALO)
    before, after = pl.ds(0, HALO), pl.ds(HALO + ROWS, HALO)
    halo = [
        links.send(o_m.at[last, :], o_m.at[before, :], **on_wire(1)),
        links.send(o_m.at[first, :], o_m.at[after, :], **on_wire(-1)),
    ]

    def coupling(dst, j, k_start):
        @pl.loop(0, 2)
        def _(t):
            dst[:, at(j * 512 + t * TILE, TILE)] = mm(ot_m[...], pr[:, at(k_start + j * 512 + t * TILE, TILE)])

    to_core = []
    for j in range(2):
        get_pr[j].wait()
        coupling(core_tx, j, other * HALF)
        part = pl.ds(j * 512, 512)
        to_core.append(links.send(core_tx.at[:, part], core_rx.at[:, part], core=other))
    for j in range(2):
        get_pr[2 + j].wait()
        coupling(acc, j, core * HALF)

    first_axis, second_axis = ("x", "y"), ("y", "x")

    got1 = []
    for lane in range(LANES):
        part = pl.ds(lane * 512, 512)
        to_core[lane].wait_recv()
        acc[:, part] += core_rx[:, part]
        axis = first_axis[lane]
        got1.append([
            links.send(
                acc.at[:, at(lane * 512 + lax.rem(at_axis[axis] + d, SIDE) * BLK, BLK)],
                rx1.at[lane, d - 1],
                **step(axis, d),
            )
            for d in (1, 2, 3)
        ])

    get_h.wait()
    for copy in halo:
        copy.wait_recv()

    @pl.loop(0, ROWS // BLK)
    def _(i):
        blocks = near(o_m, i)
        total = mm(hv[i, 0], blocks[2])
        for s in (1, 2):
            total = total + mm(hv[i, s], pick(blocks, off[i, s]))
        band[at(i * BLK, BLK), :] = total

    got2 = []
    for lane in range(LANES):
        axis = second_axis[lane]
        for copy in got1[lane]:
            copy.wait_recv()
        mine = acc[:, at(lane * 512 + at_axis[first_axis[lane]] * BLK, BLK)]
        s1[lane] = (mine + rx1[lane, 0]) + (rx1[lane, 1] + rx1[lane, 2])
        got2.append([
            links.send(
                s1.at[lane, at(lax.rem(at_axis[axis] + d, SIDE) * 64, 64), :],
                rx2.at[lane, d - 1],
                **step(axis, d),
            )
            for d in (1, 2, 3)
        ])
    got3 = []
    for lane in range(LANES):
        for copy in got2[lane]:
            copy.wait_recv()
        mine = s1[lane, at(at_axis[second_axis[lane]] * 64, 64), :]
        s2[lane] = (mine + rx2[lane, 0]) + (rx2[lane, 1] + rx2[lane, 2])
        got3.append([
            links.send(
                s2.at[lane, at(lax.rem(zh + d, ZHI) * 16, 16), :],
                rx3.at[lane, d - 1],
                **step("zh", d),
            )
            for d in (1, 2, 3)
        ])

    def k_cols(lane):
        return at(core * HALF + lane * 512 + at_axis[first_axis[lane]] * BLK, BLK)

    def c_rows(lane):
        return at(at_axis[second_axis[lane]] * 64, 64)

    got4 = []
    for lane in range(LANES):
        for copy in got3[lane]:
            copy.wait_recv()
        mine = s2[lane, at(zh * 16, 16), :]
        piece = (mine + rx3[lane, 0]) + (rx3[lane, 1] + rx3[lane, 2])
        rows = at(at_axis[second_axis[lane]] * 64 + zh * 16, 16)
        ct[0, rows, k_cols(lane)] = piece.astype(BF16)
        got4.append([
            links.send(ct.at[0, rows, k_cols(lane)], ct.at[d % 2, rows, k_cols(lane)], **along_z(d))
            for d in range(1, ZALL)
        ])
    got5 = []
    for lane in range(LANES):
        for copy in got4[lane]:
            copy.wait_recv()
        block = ct.at[:, c_rows(lane), k_cols(lane)]
        got5.append([links.send(block, block, **step(second_axis[lane], d)) for d in (1, 2, 3)])
    got6 = []
    for lane in range(LANES):
        for copy in got5[lane]:
            copy.wait_recv()
        block = ct.at[:, :, k_cols(lane)]
        got6.append([links.send(block, block, **step(first_axis[lane], d)) for d in (1, 2, 3)])

    def summed(q, crx, part_acc, rx_a, sum_a, rx_b, z_b, res):
        mine_cols, other_cols = at(core * BLK, BLK), at(other * BLK, BLK)
        copy = links.send(q.at[:, other_cols], crx, core=other)
        yield
        copy.wait_recv()
        part_acc[...] = q[:, mine_cols] + crx[...]
        got = []
        for lane in range(LANES):
            axis = first_axis[lane]
            got.append([
                links.send(
                    part_acc.at[at(lane * 256 + lax.rem(at_axis[axis] + d, SIDE) * 64, 64), :],
                    rx_a.at[lane, d - 1],
                    **step(axis, d),
                )
                for d in (1, 2, 3)
            ])
        yield
        got_b = []
        for lane in range(LANES):
            for copy in got[lane]:
                copy.wait_recv()
            mine = part_acc[at(lane * 256 + at_axis[first_axis[lane]] * 64, 64), :]
            sum_a[lane] = (mine + rx_a[lane, 0]) + (rx_a[lane, 1] + rx_a[lane, 2])
            axis = second_axis[lane]
            got_b.append([
                links.send(
                    sum_a.at[lane, at(lax.rem(at_axis[axis] + d, SIDE) * 16, 16), :],
                    rx_b.at[lane, d - 1],
                    **step(axis, d),
                )
                for d in (1, 2, 3)
            ])
        yield
        got_z = []
        for lane in range(LANES):
            for copy in got_b[lane]:
                copy.wait_recv()
            mine = sum_a[lane, at(at_axis[second_axis[lane]] * 16, 16), :]
            z_b[lane, zh] = (mine + rx_b[lane, 0]) + (rx_b[lane, 1] + rx_b[lane, 2])
            got_z.append([links.send(z_b.at[lane, zh], z_b.at[lane, zh], **step("zh", d)) for d in (1, 2, 3)])
        yield
        got_g = []
        for lane in range(LANES):
            for copy in got_z[lane]:
                copy.wait_recv()
            rows = at(lane * 256 + at_axis[first_axis[lane]] * 64 + at_axis[second_axis[lane]] * 16, 16)
            res[rows, mine_cols] = (z_b[lane, 0] + z_b[lane, 1]) + (z_b[lane, 2] + z_b[lane, 3])
            block = res.at[rows, mine_cols]
            got_g.append([links.send(block, block, **step(second_axis[lane], d)) for d in (1, 2, 3)])
        yield
        got_h = []
        for lane in range(LANES):
            for copy in got_g[lane]:
                copy.wait_recv()
            block = res.at[at(lane * 256 + at_axis[first_axis[lane]] * 64, 64), mine_cols]
            got_h.append([links.send(block, block, **step(first_axis[lane], d)) for d in (1, 2, 3)])
        yield
        for lane in range(LANES):
            for copy in got_h[lane]:
                copy.wait_recv()
        block = res.at[:, mine_cols]
        copy = links.send(block, block, core=other)
        yield
        copy.wait_recv()
        yield

    swap.wait_recv()
    halo_o = [
        links.send(o_o.at[last, :], o_o.at[before, :], **on_wire(1)),
        links.send(o_o.at[first, :], o_o.at[after, :], **on_wire(-1)),
    ]
    turn(o_o, ot_o)
    s_q[:COLS, :] = mm(ot_m[...], o_m[own, :])
    s_q[COLS:, :] = mm(ot_o[...], o_m[own, :])
    s_sum = summed(s_q, s_crx, s_acc, s_rx1, s_s1, s_rx2, s_z, s_res)
    next(s_sum)

    got7 = []
    for lane in range(LANES):
        for copy in got6[lane]:
            copy.wait_recv()
        block = ct.at[:, :, at(core * HALF + lane * 512, 512)]
        got7.append(links.send(block, block, core=other))
    next(s_sum)
    for copy in got7:
        copy.wait_recv()
    get_pl.wait()

    c_q[...] = jnp.zeros_like(c_q)

    @pl.loop(0, ROWS // TILE)
    def _(t):
        rows = at(t * TILE, TILE)
        image = band[rows, :] + mm_nt(plv[rows, :], ct[0])
        hi, lo = split(image)
        c_q[:COLS, :] += mm(ot_m[:, rows], hi) + mm(ot_m[:, rows], lo)
        c_q[COLS:, :] += mm(ot_o[:, rows], hi) + mm(ot_o[:, rows], lo)

    c_sum = summed(c_q, c_crx, c_acc, c_rx1, c_s1, c_rx2, c_z, c_res)
    next(c_sum)
    for _ in range(6):
        next(s_sum)
        next(c_sum)

    for copy in halo_o:
        copy.wait_recv()
    scale = 1.0 / TOTAL
    row = lax.broadcasted_iota(jnp.int32, (COLS, COLS), 0)
    col = lax.broadcasted_iota(jnp.int32, (COLS, COLS), 1)
    m_m = jnp.where(row == col, 2.0, 0.0) - s_res[:COLS, :] * scale
    m_o = 0.0 - s_res[COLS:, :] * scale
    mm_hi, mm_lo = split(m_m)
    mo_hi, mo_lo = split(m_o)
    tm_hi, tm_lo = split(m_m.T)
    to_hi, to_lo = split(m_o.T)

    @pl.loop(0, (ROWS + 2 * HALO) // TILE)
    def _(t):
        rows = at(t * TILE, TILE)
        a, b = o_m[rows, :], o_o[rows, :]
        y = (mm(a, mm_hi) + mm(b, mo_hi)) + (mm(a, mm_lo) + mm(b, mo_lo))
        y_hi[rows, :], y_lo[rows, :] = split(y)

    @pl.loop(0, KDIM // TILE)
    def _(t):
        cols = at(t * TILE, TILE)
        a, b = ct[0, :, cols], ct[1, :, cols]
        d = (mm(tm_hi, a) + mm(to_hi, b)) + (mm(tm_lo, a) + mm(to_lo, b))
        d_hi[:, cols], d_lo[:, cols] = split(d)

    @pl.loop(0, ROWS // BLK)
    def _(i):
        total = None
        for src in (y_lo, y_hi):
            blocks = near(src, i)
            term = mm(hv[i, 0], blocks[2])
            for s in (1, 2):
                term = term + mm(hv[i, s], pick(blocks, off[i, s]))
            total = term if total is None else total + term
        out[at(i * BLK, BLK), :] = total

    @pl.loop(0, ROWS // TILE)
    def _(t):
        rows = at(t * TILE, TILE)
        out[rows, :] += mm_nt(plv[rows, :], d_hi[...]) + mm_nt(plv[rows, :], d_lo[...])

    next(c_sum)
    xm_hi, xm_lo = split(c_res[:COLS, :] * scale)
    xo_hi, xo_lo = split(c_res[COLS:, :] * scale)

    @pl.loop(0, ROWS // TILE)
    def _(t):
        rows = at(t * TILE, TILE)
        inner = pl.ds(pl.multiple_of(HALO + t * TILE, TILE), TILE)
        a, b = o_m[inner, :], o_o[inner, :]
        out[rows, :] -= (mm(a, xm_hi) + mm(b, xo_hi)) + (mm(a, xm_lo) + mm(b, xo_lo))

    links.finish()


def body(hamiltonian, offsets, phase_left, phase_right, orbitals):
    def sums():
        return [
            pltpu.VMEM((512, 256), F32),
            pltpu.VMEM((512, 128), F32),
            pltpu.VMEM((512, 128), F32),
            pltpu.VMEM((2, 3, 64, 128), F32),
            pltpu.VMEM((2, 64, 128), F32),
            pltpu.VMEM((2, 3, 16, 128), F32),
            pltpu.VMEM((2, 4, 16, 128), F32),
            pltpu.VMEM((512, 256), F32),
        ]

    hbm = pl.BlockSpec(memory_space=pl.ANY)
    return pl.pallas_call(
        kernel,
        out_shape=jax.ShapeDtypeStruct((ROWS, COLS), F32),
        in_specs=[hbm, pl.BlockSpec(memory_space=pltpu.SMEM), hbm, hbm, hbm],
        out_specs=pl.BlockSpec(memory_space=pltpu.VMEM),
        scratch_shapes=[
            pltpu.VMEM((ROWS + 2 * HALO, COLS), BF16),
            pltpu.VMEM((ROWS + 2 * HALO, COLS), BF16),
            pltpu.VMEM((COLS, ROWS), BF16),
            pltpu.VMEM((COLS, ROWS), BF16),
            pltpu.VMEM((ROWS, KDIM), BF16),
            pltpu.VMEM((ROWS, KDIM), BF16),
            pltpu.VMEM((16, 3, BLK, BLK), BF16),
            pltpu.VMEM((COLS, HALF), F32),
            pltpu.VMEM((COLS, HALF), F32),
            pltpu.VMEM((COLS, HALF), F32),
            pltpu.VMEM((2, 3, 256, 128), F32),
            pltpu.VMEM((2, 256, 128), F32),
            pltpu.VMEM((2, 3, 64, 128), F32),
            pltpu.VMEM((2, 64, 128), F32),
            pltpu.VMEM((2, 3, 16, 128), F32),
            pltpu.VMEM((2, COLS, KDIM), BF16),
            pltpu.VMEM((ROWS, COLS), F32),
            *sums(),
            *sums(),
            pltpu.VMEM((COLS, KDIM), BF16),
            pltpu.VMEM((COLS, KDIM), BF16),
            pltpu.VMEM((ROWS + 2 * HALO, COLS), BF16),
            pltpu.VMEM((ROWS + 2 * HALO, COLS), BF16),
            pltpu.SemaphoreType.DMA((8,)),
            pltpu.SemaphoreType.DMA((N_SEMS,)),
            pltpu.SemaphoreType.DMA((N_SEMS,)),
        ],
        compiler_params=pltpu.CompilerParams(
            collective_id=0, has_side_effects=True, vmem_limit_bytes=58 << 20
        ),
        cost_estimate=pl.CostEstimate(flops=16 * 10**9, bytes_accessed=20 * 2**20, transcendentals=0),
    )(hamiltonian, offsets, phase_left, phase_right, orbitals)


def solution(mesh):
    finer = Mesh(mesh.devices.reshape(SIDE, ZHI, SIDE, 2, mesh.shape["col"]), AXES)
    in_specs = (
        P(WIRE, None, None, None),
        P(WIRE, None),
        P(WIRE, None),
        P(WIRE, None),
        P(WIRE, "zl"),
    )
    return jax.shard_map(body, mesh=finer, in_specs=in_specs, out_specs=P(WIRE, "zl"), check_vma=False)
```

```python
import jax
import jax.numpy as jnp
from jax import lax
from jax.experimental import pallas as pl
from jax.experimental.pallas import tpu as pltpu
from jax.sharding import Mesh
from jax.sharding import PartitionSpec as P

F32, BF16 = jnp.float32, jnp.bfloat16
MESH = pl.DeviceIdType.MESH
AXES = ("x", "zh", "y", "core", "zl")
WIRE = ("x", "zh", "y", "core")
SIDE, ZHI, ZALL = 4, 4, 8
LANES = 2
HALO, ROWS, COLS, KDIM, BLK = 256, 2048, 256, 2048, 128
HALF = KDIM // 2
TOTAL = 262144
TILE = 256


def mm(a, b):
    return jnp.dot(a, b, preferred_element_type=F32)


def mm_nt(a, b):
    return lax.dot_general(a, b, (((1,), (1,)), ((), ())), preferred_element_type=F32)


def split(v):
    hi = v.astype(BF16)
    return hi, (v - hi.astype(F32)).astype(BF16)


def at(start, size):
    return pl.ds(pl.multiple_of(start, size), size)


def near(src, i):
    return [src[at((i + r) * BLK, BLK), :] for r in range(5)]


def pick(blocks, shift):
    chosen = blocks[2]
    for r in (0, 1, 3, 4):
        chosen = jnp.where(shift == r - 2, blocks[r], chosen)
    return chosen


class Links:
    def __init__(self, send_sems, recv_sems):
        self.send_sems, self.recv_sems, self.started = send_sems, recv_sems, []

    def send(self, src, dst, **where):
        i = len(self.started)
        copy = pltpu.make_async_remote_copy(
            src_ref=src,
            dst_ref=dst,
            send_sem=self.send_sems.at[i],
            recv_sem=self.recv_sems.at[i],
            device_id=where,
            device_id_type=MESH,
        )
        copy.start()
        self.started.append(copy)
        return copy

    def finish(self):
        for copy in self.started:
            copy.wait_send()


N_SEMS = 160


def kernel(
    ham, off, phase_l, phase_r, orb, base, cols_o, cross,
    o_m, o_o, ot, pr, plv, hv,
    core_tx, core_rx, acc, rx1, s1, rx2, s2, rx3, ct, image, im_hi, im_lo,
    s_q, s_crx, s_acc, s_rx1, s_s1, s_rx2, s_z, s_res,
    c_q, c_crx, c_acc, c_rx1, c_s1, c_rx2, c_z, c_res,
    d2, y_hi, y_lo, rest,
    load_sems, send_sems, recv_sems,
):
    at_axis = {a: lax.axis_index(a) for a in AXES}
    core, zl, zh = at_axis["core"], at_axis["zl"], at_axis["zh"]
    other = 1 - core
    z = zh * 2 + zl
    wire = ((at_axis["x"] * ZHI + zh) * SIDE + at_axis["y"]) * 2 + core
    n_wire = SIDE * ZHI * SIDE * 2

    def step(axis, d):
        return {axis: lax.rem(at_axis[axis] + d, SIDE)}

    def along_z(d):
        there = lax.rem(z + d, ZALL)
        return {"zh": there // 2, "zl": lax.rem(there, 2)}

    def on_wire(d):
        w = lax.rem(wire + d + n_wire, n_wire)
        return {
            "x": w // (ZHI * SIDE * 2),
            "zh": lax.rem(w // (SIDE * 2), ZHI),
            "y": lax.rem(w // 2, SIDE),
            "core": lax.rem(w, 2),
        }

    links = Links(send_sems, recv_sems)
    own = pl.ds(HALO, ROWS)

    def load(src, dst, i):
        copy = pltpu.make_async_copy(src, dst, load_sems.at[i])
        copy.start()
        return copy

    get_o = load(orb, o_m.at[own, :], 0)
    get_pr = []
    for i in range(4):
        start = (other if i < 2 else core) * HALF + (i % 2) * 512
        cols = at(start, 512)
        get_pr.append(load(phase_r.at[:, cols], pr.at[:, cols], 1 + i))
    barrier = pltpu.get_barrier_semaphore()
    greeted = [step(a, d) for a in ("x", "y") for d in (1, 2, 3)]
    greeted += [along_z(d) for d in range(1, ZALL)]
    greeted += [{"core": other}, on_wire(1), on_wire(-1)]
    for where in greeted:
        pl.semaphore_signal(barrier, inc=1, device_id=where, device_id_type=MESH)
    get_o.wait()

    def turn(src, top):
        @pl.loop(0, ROWS // 512)
        def _(t):
            inner = pl.ds(pl.multiple_of(HALO + t * 512, TILE), 512)
            ot[top : top + COLS, at(t * 512, 512)] = src[inner, :].T

    turn(o_m, 0)

    def coupling(dst, j, k_start):
        dst[:, j * 512 : (j + 1) * 512] = mm(ot[:COLS, :], pr[:, at(k_start + j * 512, 512)])

    get_pr[0].wait()
    coupling(core_tx, 0, other * HALF)
    pl.semaphore_wait(barrier, len(greeted))

    def core_send(j):
        part = pl.ds(j * 512, 512)
        return links.send(core_tx.at[:, part], core_rx.at[:, part], core=other)

    last, first = pl.ds(ROWS, HALO), pl.ds(HALO, HALO)
    before, after = pl.ds(0, HALO), pl.ds(HALO + ROWS, HALO)
    to_core = [core_send(0)]
    halo = [
        links.send(o_m.at[last, :], o_m.at[before, :], **on_wire(1)),
        links.send(o_m.at[first, :], o_m.at[after, :], **on_wire(-1)),
    ]
    swap = links.send(o_m.at[own, :], o_o.at[own, :], zl=1 - zl)
    get_pr[1].wait()
    coupling(core_tx, 1, other * HALF)
    to_core.append(core_send(1))
    for j in range(2):
        get_pr[2 + j].wait()
        coupling(acc, j, core * HALF)
    get_h = load(ham, hv, 5)
    get_pl = load(phase_l, plv, 6)

    first_axis, second_axis = ("x", "y"), ("y", "x")
    got1 = []
    for lane in range(LANES):
        part = pl.ds(lane * 512, 512)
        to_core[lane].wait_recv()
        acc[:, part] += core_rx[:, part]
        axis = first_axis[lane]
        got1.append([
            links.send(
                acc.at[:, at(lane * 512 + lax.rem(at_axis[axis] + d, SIDE) * BLK, BLK)],
                rx1.at[lane, d - 1],
                **step(axis, d),
            )
            for d in (1, 2, 3)
        ])
    got2 = []
    for lane in range(LANES):
        axis = second_axis[lane]
        for copy in got1[lane]:
            copy.wait_recv()
        mine = acc[:, at(lane * 512 + at_axis[first_axis[lane]] * BLK, BLK)]
        s1[lane] = (mine + rx1[lane, 0]) + (rx1[lane, 1] + rx1[lane, 2])
        got2.append([
            links.send(
                s1.at[lane, at(lax.rem(at_axis[axis] + d, SIDE) * 64, 64), :],
                rx2.at[lane, d - 1],
                **step(axis, d),
            )
            for d in (1, 2, 3)
        ])
    got3 = []
    for lane in range(LANES):
        for copy in got2[lane]:
            copy.wait_recv()
        mine = s1[lane, at(at_axis[second_axis[lane]] * 64, 64), :]
        s2[lane] = (mine + rx2[lane, 0]) + (rx2[lane, 1] + rx2[lane, 2])
        got3.append([
            links.send(
                s2.at[lane, at(lax.rem(zh + d, ZHI) * 16, 16), :],
                rx3.at[lane, d - 1],
                **step("zh", d),
            )
            for d in (1, 2, 3)
        ])

    def k_cols(lane):
        return at(core * HALF + lane * 512 + at_axis[first_axis[lane]] * BLK, BLK)

    def c_rows(lane):
        return at(at_axis[second_axis[lane]] * 64, 64)

    got4 = []
    for lane in range(LANES):
        for copy in got3[lane]:
            copy.wait_recv()
        mine = s2[lane, at(zh * 16, 16), :]
        piece = (mine + rx3[lane, 0]) + (rx3[lane, 1] + rx3[lane, 2])
        rows = at(at_axis[second_axis[lane]] * 64 + zh * 16, 16)
        ct[0, rows, k_cols(lane)] = piece.astype(BF16)
        got4.append([
            links.send(ct.at[0, rows, k_cols(lane)], ct.at[d % 2, rows, k_cols(lane)], **along_z(d))
            for d in range(1, ZALL)
        ])
    got5 = []
    for lane in range(LANES):
        for copy in got4[lane]:
            copy.wait_recv()
        block = ct.at[:, c_rows(lane), k_cols(lane)]
        got5.append([links.send(block, block, **step(second_axis[lane], d)) for d in (1, 2, 3)])

    def summed(q, crx, part_acc, rx_a, sum_a, rx_b, z_b, res):
        mine_cols, other_cols = at(core * BLK, BLK), at(other * BLK, BLK)
        copy = links.send(q.at[:, other_cols], crx, core=other)
        yield
        copy.wait_recv()
        part_acc[...] = q[:, mine_cols] + crx[...]
        got = []
        for lane in range(LANES):
            axis = first_axis[lane]
            got.append([
                links.send(
                    part_acc.at[at(lane * 256 + lax.rem(at_axis[axis] + d, SIDE) * 64, 64), :],
                    rx_a.at[lane, d - 1],
                    **step(axis, d),
                )
                for d in (1, 2, 3)
            ])
        yield
        got_b = []
        for lane in range(LANES):
            for copy in got[lane]:
                copy.wait_recv()
            mine = part_acc[at(lane * 256 + at_axis[first_axis[lane]] * 64, 64), :]
            sum_a[lane] = (mine + rx_a[lane, 0]) + (rx_a[lane, 1] + rx_a[lane, 2])
            axis = second_axis[lane]
            got_b.append([
                links.send(
                    sum_a.at[lane, at(lax.rem(at_axis[axis] + d, SIDE) * 16, 16), :],
                    rx_b.at[lane, d - 1],
                    **step(axis, d),
                )
                for d in (1, 2, 3)
            ])
        yield
        got_z = []
        for lane in range(LANES):
            for copy in got_b[lane]:
                copy.wait_recv()
            mine = sum_a[lane, at(at_axis[second_axis[lane]] * 16, 16), :]
            z_b[lane, zh] = (mine + rx_b[lane, 0]) + (rx_b[lane, 1] + rx_b[lane, 2])
            got_z.append([links.send(z_b.at[lane, zh], z_b.at[lane, zh], **step("zh", d)) for d in (1, 2, 3)])
        yield
        got_g = []
        for lane in range(LANES):
            for copy in got_z[lane]:
                copy.wait_recv()
            rows = at(lane * 256 + at_axis[first_axis[lane]] * 64 + at_axis[second_axis[lane]] * 16, 16)
            res[rows, mine_cols] = (z_b[lane, 0] + z_b[lane, 1]) + (z_b[lane, 2] + z_b[lane, 3])
            block = res.at[rows, mine_cols]
            got_g.append([links.send(block, block, **step(second_axis[lane], d)) for d in (1, 2, 3)])
        yield
        got_h = []
        for lane in range(LANES):
            for copy in got_g[lane]:
                copy.wait_recv()
            block = res.at[at(lane * 256 + at_axis[first_axis[lane]] * 64, 64), mine_cols]
            got_h.append([links.send(block, block, **step(first_axis[lane], d)) for d in (1, 2, 3)])
        yield
        for lane in range(LANES):
            for copy in got_h[lane]:
                copy.wait_recv()
        block = res.at[:, mine_cols]
        copy = links.send(block, block, core=other)
        yield
        copy.wait_recv()
        yield

    got6 = []
    for lane in range(LANES):
        for copy in got5[lane]:
            copy.wait_recv()
        block = ct.at[:, :, k_cols(lane)]
        got6.append([links.send(block, block, **step(first_axis[lane], d)) for d in (1, 2, 3)])

    swap.wait_recv()
    put_o = load(o_o.at[own, :], cols_o, 7)
    halo_o = [
        links.send(o_o.at[last, :], o_o.at[before, :], **on_wire(1)),
        links.send(o_o.at[first, :], o_o.at[after, :], **on_wire(-1)),
    ]
    turn(o_o, COLS)
    s_q[...] = mm(ot[...], o_m[own, :])
    s_sum = summed(s_q, s_crx, s_acc, s_rx1, s_s1, s_rx2, s_z, s_res)
    next(s_sum)

    get_h.wait()
    for copy in halo:
        copy.wait_recv()

    @pl.loop(0, ROWS // BLK)
    def _(i):
        blocks = near(o_m, i)
        total = mm(hv[i, 0], blocks[2])
        for s in (1, 2):
            total = total + mm(hv[i, s], pick(blocks, off[s, i]))
        image[at(i * BLK, BLK), :] = total

    next(s_sum)
    got7 = []
    for lane in range(LANES):
        for copy in got6[lane]:
            copy.wait_recv()
        block = ct.at[:, :, at(core * HALF + lane * 512, 512)]
        got7.append(links.send(block, block, core=other))
    next(s_sum)
    get_pl.wait()

    k_mine, k_other = at(core * HALF, HALF), at(other * HALF, HALF)

    @pl.loop(0, ROWS // 1024)
    def _(t):
        rows = at(t * 1024, 1024)
        image[rows, :] += mm_nt(plv[rows, k_mine], ct[0, :, k_mine])

    for copy in got7:
        copy.wait_recv()

    @pl.loop(0, ROWS // 1024)
    def _(t):
        rows = at(t * 1024, 1024)
        im_hi[rows, :], im_lo[rows, :] = split(image[rows, :] + mm_nt(plv[rows, k_other], ct[0, :, k_other]))

    c_q[...] = mm(ot[...], im_hi[...]) + mm(ot[...], im_lo[...])
    c_sum = summed(c_q, c_crx, c_acc, c_rx1, c_s1, c_rx2, c_z, c_res)
    next(c_sum)
    next(s_sum)
    next(c_sum)
    next(s_sum)
    next(c_sum)
    next(s_sum)
    next(c_sum)
    next(s_sum)
    next(s_sum)

    scale = 1.0 / TOTAL
    row = lax.broadcasted_iota(jnp.int32, (COLS, COLS), 0)
    col = lax.broadcasted_iota(jnp.int32, (COLS, COLS), 1)
    m_m = jnp.where(row == col, 2.0, 0.0) - s_res[:COLS, :] * scale
    m_o = 0.0 - s_res[COLS:, :] * scale
    mm_hi, mm_lo = split(m_m)
    mo_hi, mo_lo = split(m_o)
    tm_hi, tm_lo = split(m_m.T)
    to_hi, to_lo = split(m_o.T)

    @pl.loop(0, KDIM // 512)
    def _(t):
        cols = at(t * 512, 512)
        a, b = ct[0, :, cols], ct[1, :, cols]
        d = (mm(tm_hi, a) + mm(to_hi, b)) + (mm(tm_lo, a) + mm(to_lo, b))
        d2[:COLS, cols], d2[COLS:, cols] = split(d)

    next(c_sum)
    for copy in halo_o:
        copy.wait_recv()

    @pl.loop(0, (ROWS + 2 * HALO) // 512)
    def _(t):
        rows = at(t * 512, 512)
        a, b = o_m[rows, :], o_o[rows, :]
        y = (mm(a, mm_hi) + mm(b, mo_hi)) + (mm(a, mm_lo) + mm(b, mo_lo))
        y_hi[rows, :], y_lo[rows, :] = split(y)

    next(c_sum)

    @pl.loop(0, ROWS // BLK)
    def _(i):
        total = None
        for src in (y_lo, y_hi):
            blocks = near(src, i)
            term = mm(hv[i, 0], blocks[2])
            for s in (1, 2):
                term = term + mm(hv[i, s], pick(blocks, off[s, i]))
            total = term if total is None else total + term
        rest[at(i * BLK, BLK), :] = total

    next(c_sum)

    @pl.loop(0, ROWS // 512)
    def _(t):
        rows = at(t * 512, 512)
        both = mm_nt(plv[rows, :], d2[...])
        rest[rows, :] += both[:, :COLS] + both[:, COLS:]

    put_base = load(rest, base, 8)
    next(c_sum)
    put_cross = load(c_res, cross, 9)
    for copy in (put_o, put_base, put_cross):
        copy.wait()
    links.finish()


def last_kernel(base, o_m, o_o, cross, out, x_hi, x_lo):
    @pl.when(pl.program_id(0) == 0)
    def _():
        x_hi[...], x_lo[...] = split(cross[...] * (1.0 / TOTAL))

    a, b = o_m[...], o_o[...]
    low = mm(a, x_lo[:COLS, :]) + mm(b, x_lo[COLS:, :])
    out[...] = base[...] - ((mm(a, x_hi[:COLS, :]) + mm(b, x_hi[COLS:, :])) + low)


def body(hamiltonian, offsets, phase_left, phase_right, orbitals):
    def sums():
        return [
            pltpu.VMEM((512, 256), F32),
            pltpu.VMEM((512, 128), F32),
            pltpu.VMEM((512, 128), F32),
            pltpu.VMEM((2, 3, 64, 128), F32),
            pltpu.VMEM((2, 64, 128), F32),
            pltpu.VMEM((2, 3, 16, 128), F32),
            pltpu.VMEM((2, 4, 16, 128), F32),
            pltpu.VMEM((512, 256), F32),
        ]

    hbm = pl.BlockSpec(memory_space=pl.ANY)
    base, cols_o, cross = pl.pallas_call(
        kernel,
        out_shape=[
            jax.ShapeDtypeStruct((ROWS, COLS), F32),
            jax.ShapeDtypeStruct((ROWS, COLS), BF16),
            jax.ShapeDtypeStruct((2 * COLS, COLS), F32),
        ],
        in_specs=[hbm, pl.BlockSpec(memory_space=pltpu.SMEM), hbm, hbm, hbm],
        out_specs=[hbm, hbm, hbm],
        scratch_shapes=[
            pltpu.VMEM((ROWS + 2 * HALO, COLS), BF16),
            pltpu.VMEM((ROWS + 2 * HALO, COLS), BF16),
            pltpu.VMEM((2 * COLS, ROWS), BF16),
            pltpu.VMEM((ROWS, KDIM), BF16),
            pltpu.VMEM((ROWS, KDIM), BF16),
            pltpu.VMEM((16, 3, BLK, BLK), BF16),
            pltpu.VMEM((COLS, HALF), F32),
            pltpu.VMEM((COLS, HALF), F32),
            pltpu.VMEM((COLS, HALF), F32),
            pltpu.VMEM((2, 3, 256, 128), F32),
            pltpu.VMEM((2, 256, 128), F32),
            pltpu.VMEM((2, 3, 64, 128), F32),
            pltpu.VMEM((2, 64, 128), F32),
            pltpu.VMEM((2, 3, 16, 128), F32),
            pltpu.VMEM((2, COLS, KDIM), BF16),
            pltpu.VMEM((ROWS, COLS), F32),
            pltpu.VMEM((ROWS, COLS), BF16),
            pltpu.VMEM((ROWS, COLS), BF16),
            *sums(),
            *sums(),
            pltpu.VMEM((2 * COLS, KDIM), BF16),
            pltpu.VMEM((ROWS + 2 * HALO, COLS), BF16),
            pltpu.VMEM((ROWS + 2 * HALO, COLS), BF16),
            pltpu.VMEM((ROWS, COLS), F32),
            pltpu.SemaphoreType.DMA((10,)),
            pltpu.SemaphoreType.DMA((N_SEMS,)),
            pltpu.SemaphoreType.DMA((N_SEMS,)),
        ],
        compiler_params=pltpu.CompilerParams(
            collective_id=0, has_side_effects=True, vmem_limit_bytes=58 << 20
        ),
        cost_estimate=pl.CostEstimate(flops=16 * 10**9, bytes_accessed=20 * 2**20, transcendentals=0),
    )(hamiltonian, offsets.T, phase_left, phase_right, orbitals)
    tile = pl.BlockSpec((512, COLS), lambda i: (i, 0))
    whole = pl.BlockSpec((2 * COLS, COLS), lambda i: (0, 0))
    return pl.pallas_call(
        last_kernel,
        grid=(ROWS // 512,),
        out_shape=jax.ShapeDtypeStruct((ROWS, COLS), F32),
        in_specs=[tile, tile, tile, whole],
        out_specs=tile,
        scratch_shapes=[pltpu.VMEM((2 * COLS, COLS), BF16), pltpu.VMEM((2 * COLS, COLS), BF16)],
        compiler_params=pltpu.CompilerParams(vmem_limit_bytes=24 << 20),
    )(base, orbitals, cols_o, cross)


def solution(mesh):
    finer = Mesh(mesh.devices.reshape(SIDE, ZHI, SIDE, 2, mesh.shape["col"]), AXES)
    in_specs = (
        P(WIRE, None, None, None),
        P(WIRE, None),
        P(WIRE, None),
        P(WIRE, None),
        P(WIRE, "zl"),
    )
    return jax.shard_map(body, mesh=finer, in_specs=in_specs, out_specs=P(WIRE, "zl"), check_vma=False)
```

```python
import jax
import jax.numpy as jnp
from jax import lax
from jax.experimental import pallas as pl
from jax.experimental.pallas import tpu as pltpu
from jax.sharding import Mesh
from jax.sharding import PartitionSpec as P

F32, BF16 = jnp.float32, jnp.bfloat16
MESH = pl.DeviceIdType.MESH
AXES = ("x", "zh", "y", "core", "zl")
WIRE = ("x", "zh", "y", "core")
SIDE, ZHI, ZALL = 4, 4, 8
LANES = 2
HALO, ROWS, COLS, KDIM, BLK = 256, 2048, 256, 2048, 128
HALF = KDIM // 2
TOTAL = 262144
TILE = 256


def mm(a, b):
    return jnp.dot(a, b, preferred_element_type=F32)


def mm_nt(a, b):
    return lax.dot_general(a, b, (((1,), (1,)), ((), ())), preferred_element_type=F32)


def split(v):
    hi = v.astype(BF16)
    return hi, (v - hi.astype(F32)).astype(BF16)


def at(start, size):
    return pl.ds(pl.multiple_of(start, size), size)


def near(src, i):
    return [src[at((i + r) * BLK, BLK), :] for r in range(5)]


def pick(blocks, shift):
    chosen = blocks[2]
    for r in (0, 1, 3, 4):
        chosen = jnp.where(shift == r - 2, blocks[r], chosen)
    return chosen


class Links:
    def __init__(self, send_sems, recv_sems):
        self.send_sems, self.recv_sems, self.started = send_sems, recv_sems, []

    def send(self, src, dst, **where):
        i = len(self.started)
        copy = pltpu.make_async_remote_copy(
            src_ref=src,
            dst_ref=dst,
            send_sem=self.send_sems.at[i],
            recv_sem=self.recv_sems.at[i],
            device_id=where,
            device_id_type=MESH,
        )
        copy.start()
        self.started.append(copy)
        return copy

    def finish(self):
        for copy in self.started:
            copy.wait_send()


N_SEMS = 160
EARLY, LATE = 256, 768


def kernel(
    ham, off, phase_l, phase_r, orb, base, cols_o, cross,
    o_m, o_o, ot, pr, plv, hv,
    core_tx, core_rx, acc, rx1, s1, rx2, s2, rx3, ct, image, im_hi, im_lo,
    s_q, s_crx, s_acc, s_rx1, s_s1, s_rx2, s_z, s_res,
    c_q, c_crx, c_acc, c_rx1, c_s1, c_rx2, c_z, c_res,
    mt, m2, d2, y2, rest,
    load_sems, send_sems, recv_sems,
):
    at_axis = {a: lax.axis_index(a) for a in AXES}
    core, zl, zh = at_axis["core"], at_axis["zl"], at_axis["zh"]
    other = 1 - core
    z = zh * 2 + zl
    wire = ((at_axis["x"] * ZHI + zh) * SIDE + at_axis["y"]) * 2 + core
    n_wire = SIDE * ZHI * SIDE * 2
    first_axis, second_axis = ("x", "y"), ("y", "x")

    def step(axis, d):
        return {axis: lax.rem(at_axis[axis] + d, SIDE)}

    def along_z(d):
        there = lax.rem(z + d, ZALL)
        return {"zh": there // 2, "zl": lax.rem(there, 2)}

    def on_wire(d):
        w = lax.rem(wire + d + n_wire, n_wire)
        return {
            "x": w // (ZHI * SIDE * 2),
            "zh": lax.rem(w // (SIDE * 2), ZHI),
            "y": lax.rem(w // 2, SIDE),
            "core": lax.rem(w, 2),
        }

    links = Links(send_sems, recv_sems)
    own = pl.ds(HALO, ROWS)

    def arrived(copies):
        for copy in copies:
            copy.wait_recv()

    def load(src, dst, i):
        copy = pltpu.make_async_copy(src, dst, load_sems.at[i])
        copy.start()
        return copy

    get_o = load(orb, o_m.at[own, :], 0)
    get_pr = []
    for i in range(4):
        start = (other if i < 2 else core) * HALF + (i % 2) * 512
        cols = at(start, 512)
        get_pr.append(load(phase_r.at[:, cols], pr.at[:, cols], 1 + i))
    barrier = pltpu.get_barrier_semaphore()
    greeted = [step(a, d) for a in ("x", "y") for d in (1, 2, 3)]
    greeted += [along_z(d) for d in range(1, ZALL)]
    greeted += [{"core": other}, on_wire(1), on_wire(-1)]
    for where in greeted:
        pl.semaphore_signal(barrier, inc=1, device_id=where, device_id_type=MESH)
    get_o.wait()

    @pl.loop(0, ROWS // 512)
    def _(t):
        inner = pl.ds(pl.multiple_of(HALO + t * 512, TILE), 512)
        ot[:COLS, at(t * 512, 512)] = o_m[inner, :].T

    def turn_half(half):
        @pl.loop(0, 2)
        def _(t):
            start = half * 1024 + t * 512
            inner = pl.ds(pl.multiple_of(HALO + start, TILE), 512)
            ot[COLS:, at(start, 512)] = o_o[inner, :].T

    def coupling(dst, j, k_start):
        dst[:, j * 512 : (j + 1) * 512] = mm(ot[:COLS, :], pr[:, at(k_start + j * 512, 512)])

    get_pr[0].wait()
    coupling(core_tx, 0, other * HALF)
    pl.semaphore_wait(barrier, len(greeted))

    def core_send(j):
        part = pl.ds(j * 512, 512)
        return links.send(core_tx.at[:, part], core_rx.at[:, part], core=other)

    def swap(start, size):
        part = pl.ds(pl.multiple_of(HALO + start, TILE), size)
        return links.send(o_m.at[part, :], o_o.at[part, :], zl=1 - zl)

    last, first = pl.ds(ROWS, HALO), pl.ds(HALO, HALO)
    before, after = pl.ds(0, HALO), pl.ds(HALO + ROWS, HALO)
    to_core = [core_send(0)]
    halo = [
        links.send(o_m.at[last, :], o_m.at[before, :], **on_wire(1)),
        links.send(o_m.at[first, :], o_m.at[after, :], **on_wire(-1)),
    ]
    swap_half = swap((1 - zl) * 1024, 1024)
    swap_early = swap(zl * 1024, EARLY)
    get_pr[1].wait()
    coupling(core_tx, 1, other * HALF)
    to_core.append(core_send(1))
    for j in range(2):
        get_pr[2 + j].wait()
        coupling(acc, j, core * HALF)
    get_h = load(ham, hv, 5)
    get_pl = load(phase_l, plv, 6)

    got1 = []
    for lane in range(LANES):
        part = pl.ds(lane * 512, 512)
        to_core[lane].wait_recv()
        acc[:, part] += core_rx[:, part]
        axis = first_axis[lane]
        got1.append([
            links.send(
                acc.at[:, at(lane * 512 + lax.rem(at_axis[axis] + d, SIDE) * BLK, BLK)],
                rx1.at[lane, d - 1],
                **step(axis, d),
            )
            for d in (1, 2, 3)
        ])
    got2 = []
    for lane in range(LANES):
        axis = second_axis[lane]
        arrived(got1[lane])
        mine = acc[:, at(lane * 512 + at_axis[first_axis[lane]] * BLK, BLK)]
        s1[lane] = (mine + rx1[lane, 0]) + (rx1[lane, 1] + rx1[lane, 2])
        got2.append([
            links.send(
                s1.at[lane, at(lax.rem(at_axis[axis] + d, SIDE) * 64, 64), :],
                rx2.at[lane, d - 1],
                **step(axis, d),
            )
            for d in (1, 2, 3)
        ])

    def summed(q, crx, part_acc, rx_a, sum_a, rx_b, z_b, res, both):
        mine_cols, other_cols = at(core * BLK, BLK), at(other * BLK, BLK)
        copy = links.send(q.at[:, other_cols], crx, core=other)
        yield
        copy.wait_recv()
        part_acc[...] = q[:, mine_cols] + crx[...]
        got = []
        for lane in range(LANES):
            axis = first_axis[lane]
            got.append([
                links.send(
                    part_acc.at[at(lane * 256 + lax.rem(at_axis[axis] + d, SIDE) * 64, 64), :],
                    rx_a.at[lane, d - 1],
                    **step(axis, d),
                )
                for d in (1, 2, 3)
            ])
        yield
        got_b = []
        for lane in range(LANES):
            arrived(got[lane])
            mine = part_acc[at(lane * 256 + at_axis[first_axis[lane]] * 64, 64), :]
            sum_a[lane] = (mine + rx_a[lane, 0]) + (rx_a[lane, 1] + rx_a[lane, 2])
            axis = second_axis[lane]
            got_b.append([
                links.send(
                    sum_a.at[lane, at(lax.rem(at_axis[axis] + d, SIDE) * 16, 16), :],
                    rx_b.at[lane, d - 1],
                    **step(axis, d),
                )
                for d in (1, 2, 3)
            ])
        yield
        got_z = []
        for lane in range(LANES):
            arrived(got_b[lane])
            mine = sum_a[lane, at(at_axis[second_axis[lane]] * 16, 16), :]
            slot = z if both and lane else zh
            z_b[lane, slot] = (mine + rx_b[lane, 0]) + (rx_b[lane, 1] + rx_b[lane, 2])
            if both and lane:
                places = [along_z(d) for d in range(1, ZALL)]
            else:
                places = [step("zh", d) for d in (1, 2, 3)]
            got_z.append([links.send(z_b.at[lane, slot], z_b.at[lane, slot], **where) for where in places])
        yield
        got_g = []
        for lane in range(LANES):
            arrived(got_z[lane])
            rows = at(lane * 256 + at_axis[first_axis[lane]] * 64 + at_axis[second_axis[lane]] * 16, 16)
            total = (z_b[lane, 0] + z_b[lane, 1]) + (z_b[lane, 2] + z_b[lane, 3])
            if both and lane:
                total = total + ((z_b[lane, 4] + z_b[lane, 5]) + (z_b[lane, 6] + z_b[lane, 7]))
            res[rows, mine_cols] = total
            block = res.at[rows, mine_cols]
            got_g.append([links.send(block, block, **step(second_axis[lane], d)) for d in (1, 2, 3)])
        yield
        got_h = []
        for lane in range(LANES):
            arrived(got_g[lane])
            block = res.at[at(lane * 256 + at_axis[first_axis[lane]] * 64, 64), mine_cols]
            got_h.append([links.send(block, block, **step(first_axis[lane], d)) for d in (1, 2, 3)])
        yield
        for lane in range(LANES):
            arrived(got_h[lane])
        block = res.at[:, mine_cols]
        copy = links.send(block, block, core=other)
        yield
        copy.wait_recv()
        yield

    swap_half.wait_recv()
    turn_half(zl)
    s_q[:COLS, :] = mm(ot[:COLS, :], o_m[own, :])
    half = pl.ds(pl.multiple_of(HALO + zl * 1024, TILE), 1024)
    ones = jnp.where(zl == 0, o_o[half, :], o_m[half, :])
    s_q[COLS:, :] = mm(ot[at(zl * COLS, COLS), at(zl * 1024, 1024)], ones)
    s_sum = summed(s_q, s_crx, s_acc, s_rx1, s_s1, s_rx2, s_z, s_res, True)
    next(s_sum)

    got3 = []
    for lane in range(LANES):
        arrived(got2[lane])
        mine = s1[lane, at(at_axis[second_axis[lane]] * 64, 64), :]
        s2[lane] = (mine + rx2[lane, 0]) + (rx2[lane, 1] + rx2[lane, 2])
        got3.append([
            links.send(
                s2.at[lane, at(lax.rem(zh + d, ZHI) * 16, 16), :],
                rx3.at[lane, d - 1],
                **step("zh", d),
            )
            for d in (1, 2, 3)
        ])
    next(s_sum)

    def k_cols(lane):
        return at(core * HALF + lane * 512 + at_axis[first_axis[lane]] * BLK, BLK)

    def c_rows(lane):
        return at(at_axis[second_axis[lane]] * 64, 64)

    got4 = []
    for lane in range(LANES):
        arrived(got3[lane])
        mine = s2[lane, at(zh * 16, 16), :]
        piece = (mine + rx3[lane, 0]) + (rx3[lane, 1] + rx3[lane, 2])
        rows = at(at_axis[second_axis[lane]] * 64 + zh * 16, 16)
        ct[0, rows, k_cols(lane)] = piece.astype(BF16)
        got4.append({
            d: links.send(ct.at[0, rows, k_cols(lane)], ct.at[d % 2, rows, k_cols(lane)], **along_z(d))
            for d in (2, 4, 6, 1, 3, 5, 7)
        })
    next(s_sum)
    got5 = [[], []]

    def gather_second(side):
        for lane in range(LANES):
            arrived([got4[lane][d] for d in range(1, ZALL) if d % 2 == side])
            block = ct.at[side, c_rows(lane), k_cols(lane)]
            got5[side].append([links.send(block, block, **step(second_axis[lane], d)) for d in (1, 2, 3)])

    gather_second(0)
    next(s_sum)
    got6 = [[], []]

    def gather_first(side):
        for lane in range(LANES):
            arrived(got5[side][lane])
            block = ct.at[side, :, k_cols(lane)]
            got6[side].append([links.send(block, block, **step(first_axis[lane], d)) for d in (1, 2, 3)])

    gather_first(0)
    gather_second(1)
    next(s_sum)
    swap_late = swap(zl * 1024 + EARLY, LATE)

    get_h.wait()
    arrived(halo)

    @pl.loop(0, ROWS // BLK)
    def _(i):
        blocks = near(o_m, i)
        total = mm(hv[i, 0], blocks[2])
        for s in (1, 2):
            total = total + mm(hv[i, s], pick(blocks, off[s, i]))
        image[at(i * BLK, BLK), :] = total

    got7 = [[], []]

    def gather_core(side):
        for lane in range(LANES):
            arrived(got6[side][lane])
            block = ct.at[side, :, at(core * HALF + lane * 512, 512)]
            got7[side].append(links.send(block, block, core=other))

    gather_core(0)
    gather_first(1)
    next(s_sum)
    get_pl.wait()

    k_mine, k_other = at(core * HALF, HALF), at(other * HALF, HALF)

    @pl.loop(0, ROWS // 1024)
    def _(t):
        rows = at(t * 1024, 1024)
        image[rows, :] += mm_nt(plv[rows, k_mine], ct[0, :, k_mine])

    arrived(got7[0])

    @pl.loop(0, ROWS // 1024)
    def _(t):
        rows = at(t * 1024, 1024)
        im_hi[rows, :], im_lo[rows, :] = split(image[rows, :] + mm_nt(plv[rows, k_other], ct[0, :, k_other]))

    next(s_sum)
    gather_core(1)
    arrived([swap_early, swap_late])
    turn_half(1 - zl)
    c_q[...] = mm(ot[...], im_hi[...]) + mm(ot[...], im_lo[...])
    c_sum = summed(c_q, c_crx, c_acc, c_rx1, c_s1, c_rx2, c_z, c_res, False)
    next(c_sum)
    halo_o = [
        links.send(o_o.at[last, :], o_o.at[before, :], **on_wire(1)),
        links.send(o_o.at[first, :], o_o.at[after, :], **on_wire(-1)),
    ]
    put_o = load(o_o.at[own, :], cols_o, 7)

    next(s_sum)
    scale = 1.0 / TOTAL
    row = lax.broadcasted_iota(jnp.int32, (COLS, COLS), 0)
    col = lax.broadcasted_iota(jnp.int32, (COLS, COLS), 1)
    m_m = jnp.where(row == col, 2.0, 0.0) - s_res[:COLS, :] * scale
    s_01 = 0.0 - s_res[COLS:, :] * scale
    s_10 = s_01.T
    m_o = jnp.where(zl == 1, s_01, s_10)
    m2[0, :, :COLS], m2[0, :, COLS:] = split(m_m)
    m2[1, :, :COLS], m2[1, :, COLS:] = split(m_o)
    mt[:COLS, :COLS], mt[COLS:, :COLS] = split(m_m.T)
    mt[:COLS, COLS:], mt[COLS:, COLS:] = split(jnp.where(zl == 1, s_10, s_01))
    next(c_sum)
    arrived(got7[1])

    @pl.loop(0, KDIM // 512)
    def _(t):
        cols = at(t * 512, 512)
        both = mm(mt[:, :COLS], ct[0, :, cols]) + mm(mt[:, COLS:], ct[1, :, cols])
        d2[:COLS, cols], d2[COLS:, cols] = split(both[:COLS, :] + both[COLS:, :])

    next(c_sum)
    arrived(halo_o)

    @pl.loop(0, (ROWS + 2 * HALO) // 512)
    def _(t):
        rows = at(t * 512, 512)
        both = mm(o_m[rows, :], m2[0]) + mm(o_o[rows, :], m2[1])
        y2[rows, :COLS], y2[rows, COLS:] = split(both[:, :COLS] + both[:, COLS:])

    next(c_sum)

    @pl.loop(0, ROWS // BLK)
    def _(i):
        blocks = near(y2, i)
        both = mm(hv[i, 0], blocks[2])
        for s in (1, 2):
            both = both + mm(hv[i, s], pick(blocks, off[s, i]))
        rest[at(i * BLK, BLK), :] = both[:, :COLS] + both[:, COLS:]

    def with_left(t):
        rows = pl.ds(t * 1024, 1024)
        both = mm_nt(plv[rows, :], d2[...])
        rest[rows, :] += both[:, :COLS] + both[:, COLS:]

    with_left(0)
    next(c_sum)
    with_left(1)
    put_base = load(rest, base, 8)
    next(c_sum)
    next(c_sum)
    next(c_sum)
    put_cross = load(c_res, cross, 9)
    for copy in (put_o, put_base, put_cross):
        copy.wait()
    links.finish()


def last_kernel(base, o_m, o_o, cross, out, x_hi, x_lo):
    @pl.when(pl.program_id(0) == 0)
    def _():
        x_hi[...], x_lo[...] = split(cross[...] * (1.0 / TOTAL))

    a, b = o_m[...], o_o[...]
    low = mm(a, x_lo[:COLS, :]) + mm(b, x_lo[COLS:, :])
    out[...] = base[...] - ((mm(a, x_hi[:COLS, :]) + mm(b, x_hi[COLS:, :])) + low)


def body(hamiltonian, offsets, phase_left, phase_right, orbitals):
    def sums(depth):
        return [
            pltpu.VMEM((512, 256), F32),
            pltpu.VMEM((512, 128), F32),
            pltpu.VMEM((512, 128), F32),
            pltpu.VMEM((2, 3, 64, 128), F32),
            pltpu.VMEM((2, 64, 128), F32),
            pltpu.VMEM((2, 3, 16, 128), F32),
            pltpu.VMEM((2, depth, 16, 128), F32),
            pltpu.VMEM((512, 256), F32),
        ]

    hbm = pl.BlockSpec(memory_space=pl.ANY)
    base, cols_o, cross = pl.pallas_call(
        kernel,
        out_shape=[
            jax.ShapeDtypeStruct((ROWS, COLS), F32),
            jax.ShapeDtypeStruct((ROWS, COLS), BF16),
            jax.ShapeDtypeStruct((2 * COLS, COLS), F32),
        ],
        in_specs=[hbm, pl.BlockSpec(memory_space=pltpu.SMEM), hbm, hbm, hbm],
        out_specs=[hbm, hbm, hbm],
        scratch_shapes=[
            pltpu.VMEM((ROWS + 2 * HALO, COLS), BF16),
            pltpu.VMEM((ROWS + 2 * HALO, COLS), BF16),
            pltpu.VMEM((2 * COLS, ROWS), BF16),
            pltpu.VMEM((ROWS, KDIM), BF16),
            pltpu.VMEM((ROWS, KDIM), BF16),
            pltpu.VMEM((16, 3, BLK, BLK), BF16),
            pltpu.VMEM((COLS, HALF), F32),
            pltpu.VMEM((COLS, HALF), F32),
            pltpu.VMEM((COLS, HALF), F32),
            pltpu.VMEM((2, 3, 256, 128), F32),
            pltpu.VMEM((2, 256, 128), F32),
            pltpu.VMEM((2, 3, 64, 128), F32),
            pltpu.VMEM((2, 64, 128), F32),
            pltpu.VMEM((2, 3, 16, 128), F32),
            pltpu.VMEM((2, COLS, KDIM), BF16),
            pltpu.VMEM((ROWS, COLS), F32),
            pltpu.VMEM((ROWS, COLS), BF16),
            pltpu.VMEM((ROWS, COLS), BF16),
            *sums(ZALL),
            *sums(ZHI),
            pltpu.VMEM((2 * COLS, 2 * COLS), BF16),
            pltpu.VMEM((2, COLS, 2 * COLS), BF16),
            pltpu.VMEM((2 * COLS, KDIM), BF16),
            pltpu.VMEM((ROWS + 2 * HALO, 2 * COLS), BF16),
            pltpu.VMEM((ROWS, COLS), F32),
            pltpu.SemaphoreType.DMA((10,)),
            pltpu.SemaphoreType.DMA((N_SEMS,)),
            pltpu.SemaphoreType.DMA((N_SEMS,)),
        ],
        compiler_params=pltpu.CompilerParams(
            collective_id=0, has_side_effects=True, vmem_limit_bytes=58 << 20
        ),
        cost_estimate=pl.CostEstimate(flops=16 * 10**9, bytes_accessed=20 * 2**20, transcendentals=0),
    )(hamiltonian, offsets.T, phase_left, phase_right, orbitals)
    tile = pl.BlockSpec((512, COLS), lambda i: (i, 0))
    whole = pl.BlockSpec((2 * COLS, COLS), lambda i: (0, 0))
    return pl.pallas_call(
        last_kernel,
        grid=(ROWS // 512,),
        out_shape=jax.ShapeDtypeStruct((ROWS, COLS), F32),
        in_specs=[tile, tile, tile, whole],
        out_specs=tile,
        scratch_shapes=[pltpu.VMEM((2 * COLS, COLS), BF16), pltpu.VMEM((2 * COLS, COLS), BF16)],
        compiler_params=pltpu.CompilerParams(vmem_limit_bytes=60 << 20),
    )(base, orbitals, cols_o, cross)


def solution(mesh):
    finer = Mesh(mesh.devices.reshape(SIDE, ZHI, SIDE, 2, mesh.shape["col"]), AXES)
    in_specs = (
        P(WIRE, None, None, None),
        P(WIRE, None),
        P(WIRE, None),
        P(WIRE, None),
        P(WIRE, "zl"),
    )
    return jax.shard_map(body, mesh=finer, in_specs=in_specs, out_specs=P(WIRE, "zl"), check_vma=False)
```

```python
import jax
import jax.numpy as jnp
from jax import lax
from jax.experimental import pallas as pl
from jax.experimental.pallas import tpu as pltpu
from jax.sharding import Mesh
from jax.sharding import PartitionSpec as P

F32, BF16 = jnp.float32, jnp.bfloat16
MESH = pl.DeviceIdType.MESH
AXES = ("x", "zh", "y", "core", "zl")
WIRE = ("x", "zh", "y", "core")
SIDE, ZHI, ZALL = 4, 4, 8
LANES = 2
HALO, ROWS, COLS, KDIM, BLK = 256, 2048, 256, 2048, 128
HALF = KDIM // 2
TOTAL = 262144
TILE = 256


def mm(a, b):
    return jnp.dot(a, b, preferred_element_type=F32)


def mm_nt(a, b):
    return lax.dot_general(a, b, (((1,), (1,)), ((), ())), preferred_element_type=F32)


def split(v):
    hi = v.astype(BF16)
    return hi, (v - hi.astype(F32)).astype(BF16)


def at(start, size):
    return pl.ds(pl.multiple_of(start, size), size)


def near(src, i):
    return [src[at((i + r) * BLK, BLK), :] for r in range(5)]


def banded(h, blocks, shifts):
    left = jnp.concatenate([h[0], h[1], h[2]], axis=1)
    right = jnp.concatenate([blocks[2], pick(blocks, shifts[0]), pick(blocks, shifts[1])], axis=0)
    return mm(left, right)


def pick(blocks, shift):
    chosen = blocks[2]
    for r in (0, 1, 3, 4):
        chosen = jnp.where(shift == r - 2, blocks[r], chosen)
    return chosen


class Links:
    def __init__(self, send_sems, recv_sems):
        self.send_sems, self.recv_sems, self.started = send_sems, recv_sems, []

    def send(self, src, dst, **where):
        i = len(self.started)
        copy = pltpu.make_async_remote_copy(
            src_ref=src,
            dst_ref=dst,
            send_sem=self.send_sems.at[i],
            recv_sem=self.recv_sems.at[i],
            device_id=where,
            device_id_type=MESH,
        )
        copy.start()
        self.started.append(copy)
        return copy

    def finish(self):
        for copy in self.started:
            copy.wait_send()


N_SEMS = 160
EARLY, LATE = 256, 768


def kernel(
    ham, off, phase_l, phase_r, orb, base, cols_o, cross,
    o_m, o_o, ot, pr, plv, hv,
    core_tx, core_rx, acc, rx1, s1, rx2, s2, rx3, ct, image, im_hi, im_lo,
    s_q, s_crx, s_acc, s_rx1, s_s1, s_rx2, s_z, s_res,
    c_q, c_crx, c_acc, c_rx1, c_s1, c_rx2, c_z, c_res,
    mt, m2, d2, y2, rest,
    load_sems, send_sems, recv_sems,
):
    at_axis = {a: lax.axis_index(a) for a in AXES}
    core, zl, zh = at_axis["core"], at_axis["zl"], at_axis["zh"]
    other = 1 - core
    z = zh * 2 + zl
    wire = ((at_axis["x"] * ZHI + zh) * SIDE + at_axis["y"]) * 2 + core
    n_wire = SIDE * ZHI * SIDE * 2
    first_axis, second_axis = ("x", "y"), ("y", "x")

    def step(axis, d):
        return {axis: lax.rem(at_axis[axis] + d, SIDE)}

    def along_z(d):
        there = lax.rem(z + d, ZALL)
        return {"zh": there // 2, "zl": lax.rem(there, 2)}

    def on_wire(d):
        w = lax.rem(wire + d + n_wire, n_wire)
        return {
            "x": w // (ZHI * SIDE * 2),
            "zh": lax.rem(w // (SIDE * 2), ZHI),
            "y": lax.rem(w // 2, SIDE),
            "core": lax.rem(w, 2),
        }

    links = Links(send_sems, recv_sems)
    own = pl.ds(HALO, ROWS)

    def arrived(copies):
        for copy in copies:
            copy.wait_recv()

    def load(src, dst, i):
        copy = pltpu.make_async_copy(src, dst, load_sems.at[i])
        copy.start()
        return copy

    get_o = load(orb, o_m.at[own, :], 0)
    get_pr = []
    for i in range(4):
        start = (other if i < 2 else core) * HALF + (i % 2) * 512
        cols = at(start, 512)
        get_pr.append(load(phase_r.at[:, cols], pr.at[:, cols], 1 + i))
    barrier = pltpu.get_barrier_semaphore()
    greeted = [step(a, d) for a in ("x", "y") for d in (1, 2, 3)]
    greeted += [along_z(d) for d in range(1, ZALL)]
    greeted += [{"core": other}, on_wire(1), on_wire(-1)]
    for where in greeted:
        pl.semaphore_signal(barrier, inc=1, device_id=where, device_id_type=MESH)
    get_o.wait()
    pl.semaphore_wait(barrier, len(greeted))

    def swap(start, size):
        part = pl.ds(pl.multiple_of(HALO + start, TILE), size)
        return links.send(o_m.at[part, :], o_o.at[part, :], zl=1 - zl)

    last, first = pl.ds(ROWS, HALO), pl.ds(HALO, HALO)
    before, after = pl.ds(0, HALO), pl.ds(HALO + ROWS, HALO)
    halo = [
        links.send(o_m.at[last, :], o_m.at[before, :], **on_wire(1)),
        links.send(o_m.at[first, :], o_m.at[after, :], **on_wire(-1)),
    ]
    swap_half = swap((1 - zl) * 1024, 1024)
    swap_early = swap(zl * 1024, EARLY)

    @pl.loop(0, ROWS // 512)
    def _(t):
        inner = pl.ds(pl.multiple_of(HALO + t * 512, TILE), 512)
        ot[:COLS, at(t * 512, 512)] = o_m[inner, :].T

    def turn_half(half):
        @pl.loop(0, 2)
        def _(t):
            start = half * 1024 + t * 512
            inner = pl.ds(pl.multiple_of(HALO + start, TILE), 512)
            ot[COLS:, at(start, 512)] = o_o[inner, :].T

    def coupling(dst, j, k_start):
        dst[:, j * 512 : (j + 1) * 512] = mm(ot[:COLS, :], pr[:, at(k_start + j * 512, 512)])

    to_core = []
    for j in range(2):
        get_pr[j].wait()
        coupling(core_tx, j, other * HALF)
        part = pl.ds(j * 512, 512)
        to_core.append(links.send(core_tx.at[:, part], core_rx.at[:, part], core=other))
    for j in range(2):
        get_pr[2 + j].wait()
        coupling(acc, j, core * HALF)
    get_h = load(ham, hv, 5)
    get_pl = load(phase_l, plv, 6)

    got1 = []
    for lane in range(LANES):
        part = pl.ds(lane * 512, 512)
        to_core[lane].wait_recv()
        acc[:, part] += core_rx[:, part]
        axis = first_axis[lane]
        got1.append([
            links.send(
                acc.at[:, at(lane * 512 + lax.rem(at_axis[axis] + d, SIDE) * BLK, BLK)],
                rx1.at[lane, d - 1],
                **step(axis, d),
            )
            for d in (1, 2, 3)
        ])
    got2 = []
    for lane in range(LANES):
        axis = second_axis[lane]
        arrived(got1[lane])
        mine = acc[:, at(lane * 512 + at_axis[first_axis[lane]] * BLK, BLK)]
        s1[lane] = (mine + rx1[lane, 0]) + (rx1[lane, 1] + rx1[lane, 2])
        got2.append([
            links.send(
                s1.at[lane, at(lax.rem(at_axis[axis] + d, SIDE) * 64, 64), :],
                rx2.at[lane, d - 1],
                **step(axis, d),
            )
            for d in (1, 2, 3)
        ])

    def summed(q, crx, part_acc, rx_a, sum_a, rx_b, z_b, res, both):
        mine_cols, other_cols = at(core * BLK, BLK), at(other * BLK, BLK)
        copy = links.send(q.at[:, other_cols], crx, core=other)
        yield
        copy.wait_recv()
        part_acc[...] = q[:, mine_cols] + crx[...]
        got = []
        for lane in range(LANES):
            axis = first_axis[lane]
            got.append([
                links.send(
                    part_acc.at[at(lane * 256 + lax.rem(at_axis[axis] + d, SIDE) * 64, 64), :],
                    rx_a.at[lane, d - 1],
                    **step(axis, d),
                )
                for d in (1, 2, 3)
            ])
        yield
        got_b = []
        for lane in range(LANES):
            arrived(got[lane])
            mine = part_acc[at(lane * 256 + at_axis[first_axis[lane]] * 64, 64), :]
            sum_a[lane] = (mine + rx_a[lane, 0]) + (rx_a[lane, 1] + rx_a[lane, 2])
            axis = second_axis[lane]
            got_b.append([
                links.send(
                    sum_a.at[lane, at(lax.rem(at_axis[axis] + d, SIDE) * 16, 16), :],
                    rx_b.at[lane, d - 1],
                    **step(axis, d),
                )
                for d in (1, 2, 3)
            ])
        yield
        got_z = []
        for lane in range(LANES):
            arrived(got_b[lane])
            mine = sum_a[lane, at(at_axis[second_axis[lane]] * 16, 16), :]
            slot = z if both and lane else zh
            z_b[lane, slot] = (mine + rx_b[lane, 0]) + (rx_b[lane, 1] + rx_b[lane, 2])
            if both and lane:
                places = [along_z(d) for d in range(1, ZALL)]
            else:
                places = [step("zh", d) for d in (1, 2, 3)]
            got_z.append([links.send(z_b.at[lane, slot], z_b.at[lane, slot], **where) for where in places])
        yield
        got_g = []
        for lane in range(LANES):
            arrived(got_z[lane])
            rows = at(lane * 256 + at_axis[first_axis[lane]] * 64 + at_axis[second_axis[lane]] * 16, 16)
            total = (z_b[lane, 0] + z_b[lane, 1]) + (z_b[lane, 2] + z_b[lane, 3])
            if both and lane:
                total = total + ((z_b[lane, 4] + z_b[lane, 5]) + (z_b[lane, 6] + z_b[lane, 7]))
            res[rows, mine_cols] = total
            block = res.at[rows, mine_cols]
            got_g.append([links.send(block, block, **step(second_axis[lane], d)) for d in (1, 2, 3)])
        yield
        got_h = []
        for lane in range(LANES):
            arrived(got_g[lane])
            block = res.at[at(lane * 256 + at_axis[first_axis[lane]] * 64, 64), mine_cols]
            got_h.append([links.send(block, block, **step(first_axis[lane], d)) for d in (1, 2, 3)])
        yield
        for lane in range(LANES):
            arrived(got_h[lane])
        block = res.at[:, mine_cols]
        copy = links.send(block, block, core=other)
        yield
        copy.wait_recv()
        yield

    swap_half.wait_recv()
    turn_half(zl)
    s_q[:COLS, :] = mm(ot[:COLS, :], o_m[own, :])
    half = pl.ds(pl.multiple_of(HALO + zl * 1024, TILE), 1024)
    ones = jnp.where(zl == 0, o_o[half, :], o_m[half, :])
    s_q[COLS:, :] = mm(ot[at(zl * COLS, COLS), at(zl * 1024, 1024)], ones)
    s_sum = summed(s_q, s_crx, s_acc, s_rx1, s_s1, s_rx2, s_z, s_res, True)
    next(s_sum)

    got3 = []
    for lane in range(LANES):
        arrived(got2[lane])
        mine = s1[lane, at(at_axis[second_axis[lane]] * 64, 64), :]
        s2[lane] = (mine + rx2[lane, 0]) + (rx2[lane, 1] + rx2[lane, 2])
        got3.append([
            links.send(
                s2.at[lane, at(lax.rem(zh + d, ZHI) * 16, 16), :],
                rx3.at[lane, d - 1],
                **step("zh", d),
            )
            for d in (1, 2, 3)
        ])
    next(s_sum)

    def k_cols(lane):
        return at(core * HALF + lane * 512 + at_axis[first_axis[lane]] * BLK, BLK)

    def c_rows(lane):
        return at(at_axis[second_axis[lane]] * 64, 64)

    got4 = []
    for lane in range(LANES):
        arrived(got3[lane])
        mine = s2[lane, at(zh * 16, 16), :]
        piece = (mine + rx3[lane, 0]) + (rx3[lane, 1] + rx3[lane, 2])
        rows = at(at_axis[second_axis[lane]] * 64 + zh * 16, 16)
        ct[0, rows, k_cols(lane)] = piece.astype(BF16)
        got4.append({
            d: links.send(ct.at[0, rows, k_cols(lane)], ct.at[d % 2, rows, k_cols(lane)], **along_z(d))
            for d in (2, 4, 6, 1, 3, 5, 7)
        })
    next(s_sum)
    got5 = [[], []]

    def gather_second(side):
        for lane in range(LANES):
            arrived([got4[lane][d] for d in range(1, ZALL) if d % 2 == side])
            block = ct.at[side, c_rows(lane), k_cols(lane)]
            got5[side].append([links.send(block, block, **step(second_axis[lane], d)) for d in (1, 2, 3)])

    gather_second(0)
    next(s_sum)
    got6 = [[], []]

    def gather_first(side):
        for lane in range(LANES):
            arrived(got5[side][lane])
            block = ct.at[side, :, k_cols(lane)]
            got6[side].append([links.send(block, block, **step(first_axis[lane], d)) for d in (1, 2, 3)])

    gather_first(0)
    gather_second(1)
    next(s_sum)
    swap_late = swap(zl * 1024 + EARLY, LATE)

    get_h.wait()
    arrived(halo)

    @pl.loop(0, ROWS // BLK)
    def _(i):
        image[at(i * BLK, BLK), :] = banded(hv[i], near(o_m, i), (off[1, i], off[2, i]))

    got7 = [[], []]

    def gather_core(side):
        for lane in range(LANES):
            arrived(got6[side][lane])
            block = ct.at[side, :, at(core * HALF + lane * 512, 512)]
            got7[side].append(links.send(block, block, core=other))

    gather_core(0)
    gather_first(1)
    next(s_sum)
    get_pl.wait()

    k_mine, k_other = at(core * HALF, HALF), at(other * HALF, HALF)

    @pl.loop(0, ROWS // 1024)
    def _(t):
        rows = at(t * 1024, 1024)
        image[rows, :] += mm_nt(plv[rows, k_mine], ct[0, :, k_mine])

    arrived(got7[0])

    @pl.loop(0, ROWS // 1024)
    def _(t):
        rows = at(t * 1024, 1024)
        im_hi[rows, :], im_lo[rows, :] = split(image[rows, :] + mm_nt(plv[rows, k_other], ct[0, :, k_other]))

    next(s_sum)
    gather_core(1)
    arrived([swap_early, swap_late])
    turn_half(1 - zl)
    c_q[...] = mm(ot[...], im_hi[...]) + mm(ot[...], im_lo[...])
    c_sum = summed(c_q, c_crx, c_acc, c_rx1, c_s1, c_rx2, c_z, c_res, False)
    next(c_sum)
    halo_o = [
        links.send(o_o.at[last, :], o_o.at[before, :], **on_wire(1)),
        links.send(o_o.at[first, :], o_o.at[after, :], **on_wire(-1)),
    ]
    put_o = load(o_o.at[own, :], cols_o, 7)

    next(s_sum)
    scale = 1.0 / TOTAL
    row = lax.broadcasted_iota(jnp.int32, (COLS, COLS), 0)
    col = lax.broadcasted_iota(jnp.int32, (COLS, COLS), 1)
    m_m = jnp.where(row == col, 2.0, 0.0) - s_res[:COLS, :] * scale
    s_01 = 0.0 - s_res[COLS:, :] * scale
    s_10 = s_01.T
    m_o = jnp.where(zl == 1, s_01, s_10)
    m2[0, :, :COLS], m2[0, :, COLS:] = split(m_m)
    m2[1, :, :COLS], m2[1, :, COLS:] = split(m_o)
    mt[:COLS, :COLS], mt[COLS:, :COLS] = split(m_m.T)
    mt[:COLS, COLS:], mt[COLS:, COLS:] = split(jnp.where(zl == 1, s_10, s_01))
    next(c_sum)
    arrived(got7[1])

    @pl.loop(0, KDIM // 512)
    def _(t):
        cols = at(t * 512, 512)
        both = mm(mt[:, :COLS], ct[0, :, cols]) + mm(mt[:, COLS:], ct[1, :, cols])
        d2[:COLS, cols], d2[COLS:, cols] = split(both[:COLS, :] + both[COLS:, :])

    next(c_sum)
    arrived(halo_o)

    @pl.loop(0, (ROWS + 2 * HALO) // 512)
    def _(t):
        rows = at(t * 512, 512)
        both = mm(o_m[rows, :], m2[0]) + mm(o_o[rows, :], m2[1])
        y2[rows, :COLS], y2[rows, COLS:] = split(both[:, :COLS] + both[:, COLS:])

    next(c_sum)

    @pl.loop(0, ROWS // BLK)
    def _(i):
        both = banded(hv[i], near(y2, i), (off[1, i], off[2, i]))
        rest[at(i * BLK, BLK), :] = both[:, :COLS] + both[:, COLS:]

    next(c_sum)

    def with_left(t):
        rows = pl.ds(t * 1024, 1024)
        both = mm_nt(plv[rows, :], d2[...])
        rest[rows, :] += both[:, :COLS] + both[:, COLS:]

    with_left(0)
    next(c_sum)
    with_left(1)
    put_base = load(rest, base, 8)
    next(c_sum)
    next(c_sum)
    put_cross = load(c_res, cross, 9)
    for copy in (put_o, put_base, put_cross):
        copy.wait()
    links.finish()


def last_kernel(base, o_m, o_o, cross, out, x_hi, x_lo):
    @pl.when(pl.program_id(0) == 0)
    def _():
        x_hi[...], x_lo[...] = split(cross[...] * (1.0 / TOTAL))

    a, b = o_m[...], o_o[...]
    low = mm(a, x_lo[:COLS, :]) + mm(b, x_lo[COLS:, :])
    out[...] = base[...] - ((mm(a, x_hi[:COLS, :]) + mm(b, x_hi[COLS:, :])) + low)


def body(hamiltonian, offsets, phase_left, phase_right, orbitals):
    def sums(depth):
        return [
            pltpu.VMEM((512, 256), F32),
            pltpu.VMEM((512, 128), F32),
            pltpu.VMEM((512, 128), F32),
            pltpu.VMEM((2, 3, 64, 128), F32),
            pltpu.VMEM((2, 64, 128), F32),
            pltpu.VMEM((2, 3, 16, 128), F32),
            pltpu.VMEM((2, depth, 16, 128), F32),
            pltpu.VMEM((512, 256), F32),
        ]

    hbm = pl.BlockSpec(memory_space=pl.ANY)
    base, cols_o, cross = pl.pallas_call(
        kernel,
        out_shape=[
            jax.ShapeDtypeStruct((ROWS, COLS), F32),
            jax.ShapeDtypeStruct((ROWS, COLS), BF16),
            jax.ShapeDtypeStruct((2 * COLS, COLS), F32),
        ],
        in_specs=[hbm, pl.BlockSpec(memory_space=pltpu.SMEM), hbm, hbm, hbm],
        out_specs=[hbm, hbm, hbm],
        scratch_shapes=[
            pltpu.VMEM((ROWS + 2 * HALO, COLS), BF16),
            pltpu.VMEM((ROWS + 2 * HALO, COLS), BF16),
            pltpu.VMEM((2 * COLS, ROWS), BF16),
            pltpu.VMEM((ROWS, KDIM), BF16),
            pltpu.VMEM((ROWS, KDIM), BF16),
            pltpu.VMEM((16, 3, BLK, BLK), BF16),
            pltpu.VMEM((COLS, HALF), F32),
            pltpu.VMEM((COLS, HALF), F32),
            pltpu.VMEM((COLS, HALF), F32),
            pltpu.VMEM((2, 3, 256, 128), F32),
            pltpu.VMEM((2, 256, 128), F32),
            pltpu.VMEM((2, 3, 64, 128), F32),
            pltpu.VMEM((2, 64, 128), F32),
            pltpu.VMEM((2, 3, 16, 128), F32),
            pltpu.VMEM((2, COLS, KDIM), BF16),
            pltpu.VMEM((ROWS, COLS), F32),
            pltpu.VMEM((ROWS, COLS), BF16),
            pltpu.VMEM((ROWS, COLS), BF16),
            *sums(ZALL),
            *sums(ZHI),
            pltpu.VMEM((2 * COLS, 2 * COLS), BF16),
            pltpu.VMEM((2, COLS, 2 * COLS), BF16),
            pltpu.VMEM((2 * COLS, KDIM), BF16),
            pltpu.VMEM((ROWS + 2 * HALO, 2 * COLS), BF16),
            pltpu.VMEM((ROWS, COLS), F32),
            pltpu.SemaphoreType.DMA((10,)),
            pltpu.SemaphoreType.DMA((N_SEMS,)),
            pltpu.SemaphoreType.DMA((N_SEMS,)),
        ],
        compiler_params=pltpu.CompilerParams(
            collective_id=0, has_side_effects=True, vmem_limit_bytes=58 << 20
        ),
        cost_estimate=pl.CostEstimate(flops=16 * 10**9, bytes_accessed=20 * 2**20, transcendentals=0),
    )(hamiltonian, offsets.T, phase_left, phase_right, orbitals)
    tile = pl.BlockSpec((512, COLS), lambda i: (i, 0))
    whole = pl.BlockSpec((2 * COLS, COLS), lambda i: (0, 0))
    return pl.pallas_call(
        last_kernel,
        grid=(ROWS // 512,),
        out_shape=jax.ShapeDtypeStruct((ROWS, COLS), F32),
        in_specs=[tile, tile, tile, whole],
        out_specs=tile,
        scratch_shapes=[pltpu.VMEM((2 * COLS, COLS), BF16), pltpu.VMEM((2 * COLS, COLS), BF16)],
        compiler_params=pltpu.CompilerParams(vmem_limit_bytes=60 << 20),
    )(base, orbitals, cols_o, cross)


def solution(mesh):
    finer = Mesh(mesh.devices.reshape(SIDE, ZHI, SIDE, 2, mesh.shape["col"]), AXES)
    in_specs = (
        P(WIRE, None, None, None),
        P(WIRE, None),
        P(WIRE, None),
        P(WIRE, None),
        P(WIRE, "zl"),
    )
    return jax.shard_map(body, mesh=finer, in_specs=in_specs, out_specs=P(WIRE, "zl"), check_vma=False)
```

```python
import jax
import jax.numpy as jnp
from jax import lax
from jax.experimental import pallas as pl
from jax.experimental.pallas import tpu as pltpu
from jax.sharding import Mesh
from jax.sharding import PartitionSpec as P

F32, BF16 = jnp.float32, jnp.bfloat16
MESH = pl.DeviceIdType.MESH
AXES = ("x", "zh", "y", "core", "zl")
WIRE = ("x", "zh", "y", "core")
SIDE, ZHI, ZALL = 4, 4, 8
LANES = 2
HALO, ROWS, COLS, KDIM, BLK = 256, 2048, 256, 2048, 128
HALF = KDIM // 2
TOTAL = 262144
TILE = 256


def mm(a, b):
    return jnp.dot(a, b, preferred_element_type=F32)


def mm_nt(a, b):
    return lax.dot_general(a, b, (((1,), (1,)), ((), ())), preferred_element_type=F32)


def split(v):
    hi = v.astype(BF16)
    return hi, (v - hi.astype(F32)).astype(BF16)


def at(start, size):
    return pl.ds(pl.multiple_of(start, size), size)


def near(src, i):
    return [src[at((i + r) * BLK, BLK), :] for r in range(5)]


def banded(h, blocks, shifts):
    left = jnp.concatenate([h[0], h[1], h[2]], axis=1)
    right = jnp.concatenate([blocks[2], pick(blocks, shifts[0]), pick(blocks, shifts[1])], axis=0)
    return mm(left, right)


def pick(blocks, shift):
    chosen = blocks[2]
    for r in (0, 1, 3, 4):
        chosen = jnp.where(shift == r - 2, blocks[r], chosen)
    return chosen


class Links:
    def __init__(self, send_sems, recv_sems):
        self.send_sems, self.recv_sems, self.started = send_sems, recv_sems, []

    def send(self, src, dst, **where):
        i = len(self.started)
        copy = pltpu.make_async_remote_copy(
            src_ref=src,
            dst_ref=dst,
            send_sem=self.send_sems.at[i],
            recv_sem=self.recv_sems.at[i],
            device_id=where,
            device_id_type=MESH,
        )
        copy.start()
        self.started.append(copy)
        return copy

    def finish(self):
        for copy in self.started:
            copy.wait_send()


N_SEMS = 140
EARLY, LATE = 256, 768


def kernel(
    ham, off, phase_l, phase_r, orb, base, cols_o, cross,
    o_m, o_o, ot, pr, plv, hv,
    core_tx, core_rx, acc, rx1, s1, rx2, s2, rx3, ct, b_hi, b_lo, g_o, g_hi, g_lo,
    s_q, s_crx, s_acc, s_rx1, s_s1, s_rx2, s_z, s_res,
    c_q, c_crx, c_acc, c_rx1, c_s1, c_rx2, c_z, c_res,
    mt, m2, d2, y2, rest,
    load_sems, send_sems, recv_sems,
):
    at_axis = {a: lax.axis_index(a) for a in AXES}
    core, zl, zh = at_axis["core"], at_axis["zl"], at_axis["zh"]
    other = 1 - core
    z = zh * 2 + zl
    wire = ((at_axis["x"] * ZHI + zh) * SIDE + at_axis["y"]) * 2 + core
    n_wire = SIDE * ZHI * SIDE * 2
    first_axis, second_axis = ("x", "y"), ("y", "x")

    def step(axis, d):
        return {axis: lax.rem(at_axis[axis] + d, SIDE)}

    def along_z(d):
        there = lax.rem(z + d, ZALL)
        return {"zh": there // 2, "zl": lax.rem(there, 2)}

    def on_wire(d):
        w = lax.rem(wire + d + n_wire, n_wire)
        return {
            "x": w // (ZHI * SIDE * 2),
            "zh": lax.rem(w // (SIDE * 2), ZHI),
            "y": lax.rem(w // 2, SIDE),
            "core": lax.rem(w, 2),
        }

    links = Links(send_sems, recv_sems)
    own = pl.ds(HALO, ROWS)

    def arrived(copies):
        for copy in copies:
            copy.wait_recv()

    def load(src, dst, i):
        copy = pltpu.make_async_copy(src, dst, load_sems.at[i])
        copy.start()
        return copy

    get_o = load(orb, o_m.at[own, :], 0)
    get_pr = []
    for i in range(4):
        start = (other if i < 2 else core) * HALF + (i % 2) * 512
        cols = at(start, 512)
        get_pr.append(load(phase_r.at[:, cols], pr.at[:, cols], 1 + i))
    barrier = pltpu.get_barrier_semaphore()
    greeted = [step(a, d) for a in ("x", "y") for d in (1, 2, 3)]
    greeted += [along_z(d) for d in range(1, ZALL)]
    greeted += [{"core": other}, on_wire(1), on_wire(-1)]
    for where in greeted:
        pl.semaphore_signal(barrier, inc=1, device_id=where, device_id_type=MESH)
    get_o.wait()
    pl.semaphore_wait(barrier, len(greeted))

    def swap(start, size):
        part = pl.ds(pl.multiple_of(HALO + start, TILE), size)
        return links.send(o_m.at[part, :], o_o.at[part, :], zl=1 - zl)

    last, first = pl.ds(ROWS, HALO), pl.ds(HALO, HALO)
    before, after = pl.ds(0, HALO), pl.ds(HALO + ROWS, HALO)
    halo = [
        links.send(o_m.at[last, :], o_m.at[before, :], **on_wire(1)),
        links.send(o_m.at[first, :], o_m.at[after, :], **on_wire(-1)),
    ]
    swap_half = swap((1 - zl) * 1024, 1024)
    swap_early = swap(zl * 1024, EARLY)

    @pl.loop(0, ROWS // 512)
    def _(t):
        inner = pl.ds(pl.multiple_of(HALO + t * 512, TILE), 512)
        ot[:COLS, at(t * 512, 512)] = o_m[inner, :].T

    def turn_half(half):
        @pl.loop(0, 2)
        def _(t):
            start = half * 1024 + t * 512
            inner = pl.ds(pl.multiple_of(HALO + start, TILE), 512)
            ot[COLS:, at(start, 512)] = o_o[inner, :].T

    def coupling(dst, j, k_start):
        dst[:, j * 512 : (j + 1) * 512] = mm(ot[:COLS, :], pr[:, at(k_start + j * 512, 512)])

    to_core = []
    for j in range(2):
        get_pr[j].wait()
        coupling(core_tx, j, other * HALF)
        part = pl.ds(j * 512, 512)
        to_core.append(links.send(core_tx.at[:, part], core_rx.at[:, part], core=other))
    for j in range(2):
        get_pr[2 + j].wait()
        coupling(acc, j, core * HALF)
    get_h = load(ham, hv, 5)
    get_pl = load(phase_l, plv, 6)

    got1 = []
    for lane in range(LANES):
        part = pl.ds(lane * 512, 512)
        to_core[lane].wait_recv()
        acc[:, part] += core_rx[:, part]
        axis = first_axis[lane]
        got1.append([
            links.send(
                acc.at[:, at(lane * 512 + lax.rem(at_axis[axis] + d, SIDE) * BLK, BLK)],
                rx1.at[lane, d - 1],
                **step(axis, d),
            )
            for d in (1, 2, 3)
        ])
    get_pl.wait()

    @pl.loop(0, KDIM // 512)
    def _(t):
        cols = at(t * 512, 512)
        g_hi[:COLS, cols], g_lo[:COLS, cols] = split(mm(ot[:COLS, :], plv[:, cols]))

    got2 = []
    for lane in range(LANES):
        axis = second_axis[lane]
        arrived(got1[lane])
        mine = acc[:, at(lane * 512 + at_axis[first_axis[lane]] * BLK, BLK)]
        s1[lane] = (mine + rx1[lane, 0]) + (rx1[lane, 1] + rx1[lane, 2])
        got2.append([
            links.send(
                s1.at[lane, at(lax.rem(at_axis[axis] + d, SIDE) * 64, 64), :],
                rx2.at[lane, d - 1],
                **step(axis, d),
            )
            for d in (1, 2, 3)
        ])

    def summed(q, crx, part_acc, rx_a, sum_a, rx_b, z_b, res, both):
        mine_cols, other_cols = at(core * BLK, BLK), at(other * BLK, BLK)
        copy = links.send(q.at[:, other_cols], crx, core=other)
        yield
        copy.wait_recv()
        part_acc[...] = q[:, mine_cols] + crx[...]
        got = []
        for lane in range(LANES):
            axis = first_axis[lane]
            got.append([
                links.send(
                    part_acc.at[at(lane * 256 + lax.rem(at_axis[axis] + d, SIDE) * 64, 64), :],
                    rx_a.at[lane, d - 1],
                    **step(axis, d),
                )
                for d in (1, 2, 3)
            ])
        yield
        got_b = []
        for lane in range(LANES):
            arrived(got[lane])
            mine = part_acc[at(lane * 256 + at_axis[first_axis[lane]] * 64, 64), :]
            sum_a[lane] = (mine + rx_a[lane, 0]) + (rx_a[lane, 1] + rx_a[lane, 2])
            axis = second_axis[lane]
            got_b.append([
                links.send(
                    sum_a.at[lane, at(lax.rem(at_axis[axis] + d, SIDE) * 16, 16), :],
                    rx_b.at[lane, d - 1],
                    **step(axis, d),
                )
                for d in (1, 2, 3)
            ])
        yield
        got_z = []
        for lane in range(LANES):
            arrived(got_b[lane])
            mine = sum_a[lane, at(at_axis[second_axis[lane]] * 16, 16), :]
            slot = z if both and lane else zh
            z_b[lane, slot] = (mine + rx_b[lane, 0]) + (rx_b[lane, 1] + rx_b[lane, 2])
            if both and lane:
                places = [along_z(d) for d in range(1, ZALL)]
            else:
                places = [step("zh", d) for d in (1, 2, 3)]
            got_z.append([links.send(z_b.at[lane, slot], z_b.at[lane, slot], **where) for where in places])
        yield
        got_g = []
        for lane in range(LANES):
            arrived(got_z[lane])
            rows = at(lane * 256 + at_axis[first_axis[lane]] * 64 + at_axis[second_axis[lane]] * 16, 16)
            total = (z_b[lane, 0] + z_b[lane, 1]) + (z_b[lane, 2] + z_b[lane, 3])
            if both and lane:
                total = total + ((z_b[lane, 4] + z_b[lane, 5]) + (z_b[lane, 6] + z_b[lane, 7]))
            res[rows, mine_cols] = total
            block = res.at[rows, mine_cols]
            got_g.append([links.send(block, block, **step(second_axis[lane], d)) for d in (1, 2, 3)])
        yield
        got_h = []
        for lane in range(LANES):
            arrived(got_g[lane])
            block = res.at[at(lane * 256 + at_axis[first_axis[lane]] * 64, 64), mine_cols]
            got_h.append([links.send(block, block, **step(first_axis[lane], d)) for d in (1, 2, 3)])
        yield
        for lane in range(LANES):
            arrived(got_h[lane])
        block = res.at[:, mine_cols]
        copy = links.send(block, block, core=other)
        yield
        copy.wait_recv()
        yield

    swap_half.wait_recv()
    turn_half(zl)
    s_q[:COLS, :] = mm(ot[:COLS, :], o_m[own, :])
    half = pl.ds(pl.multiple_of(HALO + zl * 1024, TILE), 1024)
    ones = jnp.where(zl == 0, o_o[half, :], o_m[half, :])
    s_q[COLS:, :] = mm(ot[at(zl * COLS, COLS), at(zl * 1024, 1024)], ones)
    s_sum = summed(s_q, s_crx, s_acc, s_rx1, s_s1, s_rx2, s_z, s_res, True)
    next(s_sum)

    got3 = []
    for lane in range(LANES):
        arrived(got2[lane])
        mine = s1[lane, at(at_axis[second_axis[lane]] * 64, 64), :]
        s2[lane] = (mine + rx2[lane, 0]) + (rx2[lane, 1] + rx2[lane, 2])
        got3.append([
            links.send(
                s2.at[lane, at(lax.rem(zh + d, ZHI) * 16, 16), :],
                rx3.at[lane, d - 1],
                **step("zh", d),
            )
            for d in (1, 2, 3)
        ])
    next(s_sum)
    half_a, half_b = at(zl * 1024, 1024), at((1 - zl) * 1024, 1024)

    @pl.loop(0, KDIM // 512)
    def _(t):
        cols = at(t * 512, 512)
        g_o[:, cols] = mm(ot[COLS:, half_a], plv[half_a, cols])


    def k_cols(lane):
        return at(core * HALF + lane * 512 + at_axis[first_axis[lane]] * BLK, BLK)

    def c_rows(lane):
        return at(at_axis[second_axis[lane]] * 64, 64)

    got4 = []
    for lane in range(LANES):
        arrived(got3[lane])
        mine = s2[lane, at(zh * 16, 16), :]
        piece = (mine + rx3[lane, 0]) + (rx3[lane, 1] + rx3[lane, 2])
        rows = at(at_axis[second_axis[lane]] * 64 + zh * 16, 16)
        ct[0, rows, k_cols(lane)] = piece.astype(BF16)
        got4.append({
            d: links.send(ct.at[0, rows, k_cols(lane)], ct.at[d % 2, rows, k_cols(lane)], **along_z(d))
            for d in (2, 4, 6, 1, 3, 5, 7)
        })
    next(s_sum)
    get_h.wait()
    arrived(halo)

    @pl.loop(0, ROWS // BLK)
    def _(i):
        rows = at(i * BLK, BLK)
        b_hi[rows, :], b_lo[rows, :] = split(banded(hv[i], near(o_m, i), (off[1, i], off[2, i])))

    got5 = [[], []]

    def gather_second(side):
        for lane in range(LANES):
            arrived([got4[lane][d] for d in range(1, ZALL) if d % 2 == side])
            block = ct.at[side, c_rows(lane), k_cols(lane)]
            got5[side].append([links.send(block, block, **step(second_axis[lane], d)) for d in (1, 2, 3)])

    gather_second(0)
    next(s_sum)
    swap_late = swap(zl * 1024 + EARLY, LATE)
    c_q[:COLS, :] = mm(ot[:COLS, :], b_hi[...]) + mm(ot[:COLS, :], b_lo[...])
    c_q[COLS:, :] = mm(ot[COLS:, half_a], b_hi[half_a, :]) + mm(ot[COLS:, half_a], b_lo[half_a, :])
    got6 = [[], []]

    def gather_first(side):
        for lane in range(LANES):
            arrived(got5[side][lane])
            block = ct.at[side, :, k_cols(lane)]
            got6[side].append([links.send(block, block, **step(first_axis[lane], d)) for d in (1, 2, 3)])

    gather_first(0)
    gather_second(1)

    got7 = [[], []]

    def gather_core(side):
        for lane in range(LANES):
            arrived(got6[side][lane])
            block = ct.at[side, :, at(core * HALF + lane * 512, 512)]
            got7[side].append(links.send(block, block, core=other))

    gather_core(0)
    gather_first(1)
    arrived([swap_early, swap_late])
    turn_half(1 - zl)

    @pl.loop(0, KDIM // 512)
    def _(t):
        cols = at(t * 512, 512)
        g_hi[COLS:, cols], g_lo[COLS:, cols] = split(g_o[:, cols] + mm(ot[COLS:, half_b], plv[half_b, cols]))

    c_q[COLS:, :] += mm(ot[COLS:, half_b], b_hi[half_b, :]) + mm(ot[COLS:, half_b], b_lo[half_b, :])
    next(s_sum)

    def with_coupling(k):
        c_q[...] += mm_nt(g_hi[:, k], ct[0, :, k]) + mm_nt(g_lo[:, k], ct[0, :, k])

    with_coupling(at(core * HALF, HALF))
    arrived(got7[0])
    with_coupling(at(other * HALF, HALF))
    c_sum = summed(c_q, c_crx, c_acc, c_rx1, c_s1, c_rx2, c_z, c_res, False)
    next(c_sum)
    halo_o = [
        links.send(o_o.at[last, :], o_o.at[before, :], **on_wire(1)),
        links.send(o_o.at[first, :], o_o.at[after, :], **on_wire(-1)),
    ]
    put_o = load(o_o.at[own, :], cols_o, 7)
    gather_core(1)
    next(s_sum)
    next(c_sum)
    next(s_sum)
    next(c_sum)
    next(s_sum)

    scale = 1.0 / TOTAL
    row = lax.broadcasted_iota(jnp.int32, (COLS, COLS), 0)
    col = lax.broadcasted_iota(jnp.int32, (COLS, COLS), 1)
    m_m = jnp.where(row == col, 2.0, 0.0) - s_res[:COLS, :] * scale
    s_01 = 0.0 - s_res[COLS:, :] * scale
    s_10 = s_01.T
    m_o = jnp.where(zl == 1, s_01, s_10)
    m2[0, :, :COLS], m2[0, :, COLS:] = split(m_m)
    m2[1, :, :COLS], m2[1, :, COLS:] = split(m_o)
    mt[:COLS, :COLS], mt[COLS:, :COLS] = split(m_m.T)
    mt[:COLS, COLS:], mt[COLS:, COLS:] = split(jnp.where(zl == 1, s_10, s_01))
    arrived(got7[1])

    @pl.loop(0, KDIM // 512)
    def _(t):
        cols = at(t * 512, 512)
        both = mm(mt[:, :COLS], ct[0, :, cols]) + mm(mt[:, COLS:], ct[1, :, cols])
        d2[:COLS, cols], d2[COLS:, cols] = split(both[:COLS, :] + both[COLS:, :])

    next(c_sum)
    arrived(halo_o)

    @pl.loop(0, (ROWS + 2 * HALO) // 512)
    def _(t):
        rows = at(t * 512, 512)
        both = mm(o_m[rows, :], m2[0]) + mm(o_o[rows, :], m2[1])
        y2[rows, :COLS], y2[rows, COLS:] = split(both[:, :COLS] + both[:, COLS:])

    @pl.loop(0, ROWS // BLK)
    def _(i):
        both = banded(hv[i], near(y2, i), (off[1, i], off[2, i]))
        rest[at(i * BLK, BLK), :] = both[:, :COLS] + both[:, COLS:]

    next(c_sum)

    def with_left(t):
        rows = pl.ds(t * 1024, 1024)
        both = mm_nt(plv[rows, :], d2[...])
        rest[rows, :] += both[:, :COLS] + both[:, COLS:]

    with_left(0)
    next(c_sum)
    with_left(1)
    put_base = load(rest, base, 8)
    next(c_sum)
    next(c_sum)
    put_cross = load(c_res, cross, 9)
    for copy in (put_o, put_base, put_cross):
        copy.wait()
    links.finish()


def last_kernel(base, o_m, o_o, cross, out, x2):
    @pl.when(pl.program_id(0) == 0)
    def _():
        x2[:, :COLS], x2[:, COLS:] = split(cross[...] * (1.0 / TOTAL))

    both = mm(o_m[...], x2[:COLS, :]) + mm(o_o[...], x2[COLS:, :])
    out[...] = base[...] - (both[:, :COLS] + both[:, COLS:])


def body(hamiltonian, offsets, phase_left, phase_right, orbitals):
    def sums(depth):
        return [
            pltpu.VMEM((512, 256), F32),
            pltpu.VMEM((512, 128), F32),
            pltpu.VMEM((512, 128), F32),
            pltpu.VMEM((2, 3, 64, 128), F32),
            pltpu.VMEM((2, 64, 128), F32),
            pltpu.VMEM((2, 3, 16, 128), F32),
            pltpu.VMEM((2, depth, 16, 128), F32),
            pltpu.VMEM((512, 256), F32),
        ]

    hbm = pl.BlockSpec(memory_space=pl.ANY)
    base, cols_o, cross = pl.pallas_call(
        kernel,
        out_shape=[
            jax.ShapeDtypeStruct((ROWS, COLS), F32),
            jax.ShapeDtypeStruct((ROWS, COLS), BF16),
            jax.ShapeDtypeStruct((2 * COLS, COLS), F32),
        ],
        in_specs=[hbm, pl.BlockSpec(memory_space=pltpu.SMEM), hbm, hbm, hbm],
        out_specs=[hbm, hbm, hbm],
        scratch_shapes=[
            pltpu.VMEM((ROWS + 2 * HALO, COLS), BF16),
            pltpu.VMEM((ROWS + 2 * HALO, COLS), BF16),
            pltpu.VMEM((2 * COLS, ROWS), BF16),
            pltpu.VMEM((ROWS, KDIM), BF16),
            pltpu.VMEM((ROWS, KDIM), BF16),
            pltpu.VMEM((16, 3, BLK, BLK), BF16),
            pltpu.VMEM((COLS, HALF), F32),
            pltpu.VMEM((COLS, HALF), F32),
            pltpu.VMEM((COLS, HALF), F32),
            pltpu.VMEM((2, 3, 256, 128), F32),
            pltpu.VMEM((2, 256, 128), F32),
            pltpu.VMEM((2, 3, 64, 128), F32),
            pltpu.VMEM((2, 64, 128), F32),
            pltpu.VMEM((2, 3, 16, 128), F32),
            pltpu.VMEM((2, COLS, KDIM), BF16),
            pltpu.VMEM((ROWS, COLS), BF16),
            pltpu.VMEM((ROWS, COLS), BF16),
            pltpu.VMEM((COLS, KDIM), F32),
            pltpu.VMEM((2 * COLS, KDIM), BF16),
            pltpu.VMEM((2 * COLS, KDIM), BF16),
            *sums(ZALL),
            *sums(ZHI),
            pltpu.VMEM((2 * COLS, 2 * COLS), BF16),
            pltpu.VMEM((2, COLS, 2 * COLS), BF16),
            pltpu.VMEM((2 * COLS, KDIM), BF16),
            pltpu.VMEM((ROWS + 2 * HALO, 2 * COLS), BF16),
            pltpu.VMEM((ROWS, COLS), F32),
            pltpu.SemaphoreType.DMA((10,)),
            pltpu.SemaphoreType.DMA((N_SEMS,)),
            pltpu.SemaphoreType.DMA((N_SEMS,)),
        ],
        compiler_params=pltpu.CompilerParams(
            collective_id=0, has_side_effects=True, vmem_limit_bytes=58 << 20
        ),
        cost_estimate=pl.CostEstimate(flops=16 * 10**9, bytes_accessed=20 * 2**20, transcendentals=0),
    )(hamiltonian, offsets.T, phase_left, phase_right, orbitals)
    tile = pl.BlockSpec((512, COLS), lambda i: (i, 0))
    whole = pl.BlockSpec((2 * COLS, COLS), lambda i: (0, 0))
    return pl.pallas_call(
        last_kernel,
        grid=(ROWS // 512,),
        out_shape=jax.ShapeDtypeStruct((ROWS, COLS), F32),
        in_specs=[tile, tile, tile, whole],
        out_specs=tile,
        scratch_shapes=[pltpu.VMEM((2 * COLS, 2 * COLS), BF16)],
        compiler_params=pltpu.CompilerParams(vmem_limit_bytes=60 << 20),
    )(base, orbitals, cols_o, cross)


def solution(mesh):
    finer = Mesh(mesh.devices.reshape(SIDE, ZHI, SIDE, 2, mesh.shape["col"]), AXES)
    in_specs = (
        P(WIRE, None, None, None),
        P(WIRE, None),
        P(WIRE, None),
        P(WIRE, None),
        P(WIRE, "zl"),
    )
    return jax.shard_map(body, mesh=finer, in_specs=in_specs, out_specs=P(WIRE, "zl"), check_vma=False)
```

```python
import jax
import jax.numpy as jnp
from jax import lax
from jax.experimental import pallas as pl
from jax.experimental.pallas import tpu as pltpu
from jax.sharding import Mesh
from jax.sharding import PartitionSpec as P

F32, BF16 = jnp.float32, jnp.bfloat16
MESH = pl.DeviceIdType.MESH
AXES = ("x", "zh", "y", "core", "zl")
WIRE = ("x", "zh", "y", "core")
SIDE, ZHI, ZALL = 4, 4, 8
LANES = 2
HALO, ROWS, COLS, KDIM, BLK = 256, 2048, 256, 2048, 128
HALF = KDIM // 2
TOTAL = 262144
TILE = 256


def mm(a, b):
    return jnp.dot(a, b, preferred_element_type=F32)


def mm_nt(a, b):
    return lax.dot_general(a, b, (((1,), (1,)), ((), ())), preferred_element_type=F32)


def split(v):
    hi = v.astype(BF16)
    return hi, (v - hi.astype(F32)).astype(BF16)


def at(start, size):
    return pl.ds(pl.multiple_of(start, size), size)


def near(src, i):
    return [src[at((i + r) * BLK, BLK), :] for r in range(5)]


def banded(h, blocks, shifts):
    left = jnp.concatenate([h[0], h[1], h[2]], axis=1)
    right = jnp.concatenate([blocks[2], pick(blocks, shifts[0]), pick(blocks, shifts[1])], axis=0)
    return mm(left, right)


def pick(blocks, shift):
    chosen = blocks[2]
    for r in (0, 1, 3, 4):
        chosen = jnp.where(shift == r - 2, blocks[r], chosen)
    return chosen


class Links:
    def __init__(self, send_sems, recv_sems):
        self.send_sems, self.recv_sems, self.started = send_sems, recv_sems, []

    def send(self, src, dst, **where):
        i = len(self.started)
        copy = pltpu.make_async_remote_copy(
            src_ref=src,
            dst_ref=dst,
            send_sem=self.send_sems.at[i],
            recv_sem=self.recv_sems.at[i],
            device_id=where,
            device_id_type=MESH,
        )
        copy.start()
        self.started.append(copy)
        return copy

    def finish(self):
        for copy in self.started:
            copy.wait_send()


N_SEMS = 140
EARLY, LATE = 256, 768


def kernel(
    ham, off, phase_l, phase_r, orb, base, cols_o, cross,
    o_m, o_o, ot, pr, plv, hv,
    core_tx, core_rx, acc, rx1, s1, rx2, s2, rx3, ct, b_hi, b_lo, g_o, g_hi, g_lo,
    s_q, s_crx, s_acc, s_rx1, s_s1, s_rx2, s_z, s_res,
    c_q, c_crx, c_acc, c_rx1, c_s1, c_rx2, c_z, c_res,
    mt, m2, d2, y2, rest,
    load_sems, send_sems, recv_sems,
):
    at_axis = {a: lax.axis_index(a) for a in AXES}
    core, zl, zh = at_axis["core"], at_axis["zl"], at_axis["zh"]
    other = 1 - core
    z = zh * 2 + zl
    wire = ((at_axis["x"] * ZHI + zh) * SIDE + at_axis["y"]) * 2 + core
    n_wire = SIDE * ZHI * SIDE * 2
    first_axis, second_axis = ("x", "y"), ("y", "x")

    def step(axis, d):
        return {axis: lax.rem(at_axis[axis] + d, SIDE)}

    def along_z(d):
        there = lax.rem(z + d, ZALL)
        return {"zh": there // 2, "zl": lax.rem(there, 2)}

    def on_wire(d):
        w = lax.rem(wire + d + n_wire, n_wire)
        return {
            "x": w // (ZHI * SIDE * 2),
            "zh": lax.rem(w // (SIDE * 2), ZHI),
            "y": lax.rem(w // 2, SIDE),
            "core": lax.rem(w, 2),
        }

    links = Links(send_sems, recv_sems)
    own = pl.ds(HALO, ROWS)

    def arrived(copies):
        for copy in copies:
            copy.wait_recv()

    def load(src, dst, i):
        copy = pltpu.make_async_copy(src, dst, load_sems.at[i])
        copy.start()
        return copy

    get_o = load(orb, o_m.at[own, :], 0)
    get_pr = []
    for i in range(4):
        start = (other if i < 2 else core) * HALF + (i % 2) * 512
        cols = at(start, 512)
        get_pr.append(load(phase_r.at[:, cols], pr.at[:, cols], 1 + i))
    barrier = pltpu.get_barrier_semaphore()
    greeted = [step(a, d) for a in ("x", "y") for d in (1, 2, 3)]
    greeted += [along_z(d) for d in range(1, ZALL)]
    greeted += [{"core": other}, on_wire(1), on_wire(-1)]
    for where in greeted:
        pl.semaphore_signal(barrier, inc=1, device_id=where, device_id_type=MESH)
    get_o.wait()
    pl.semaphore_wait(barrier, len(greeted))

    def swap(start, size):
        part = pl.ds(pl.multiple_of(HALO + start, TILE), size)
        return links.send(o_m.at[part, :], o_o.at[part, :], zl=1 - zl)

    last, first = pl.ds(ROWS, HALO), pl.ds(HALO, HALO)
    before, after = pl.ds(0, HALO), pl.ds(HALO + ROWS, HALO)
    halo = [
        links.send(o_m.at[last, :], o_m.at[before, :], **on_wire(1)),
        links.send(o_m.at[first, :], o_m.at[after, :], **on_wire(-1)),
    ]
    swap_half = swap((1 - zl) * 1024, 1024)
    swap_early = swap(zl * 1024, EARLY)

    @pl.loop(0, ROWS // 512)
    def _(t):
        inner = pl.ds(pl.multiple_of(HALO + t * 512, TILE), 512)
        ot[:COLS, at(t * 512, 512)] = o_m[inner, :].T

    def turn_half(half):
        @pl.loop(0, 2)
        def _(t):
            start = half * 1024 + t * 512
            inner = pl.ds(pl.multiple_of(HALO + start, TILE), 512)
            ot[COLS:, at(start, 512)] = o_o[inner, :].T

    def coupling(dst, j, k_start):
        dst[:, j * 512 : (j + 1) * 512] = mm(ot[:COLS, :], pr[:, at(k_start + j * 512, 512)])

    to_core = []
    for j in range(2):
        get_pr[j].wait()
        coupling(core_tx, j, other * HALF)
        part = pl.ds(j * 512, 512)
        to_core.append(links.send(core_tx.at[:, part], core_rx.at[:, part], core=other))
    for j in range(2):
        get_pr[2 + j].wait()
        coupling(acc, j, core * HALF)
    get_h = load(ham, hv, 5)
    get_pl = load(phase_l, plv, 6)

    got1 = []
    for lane in range(LANES):
        part = pl.ds(lane * 512, 512)
        to_core[lane].wait_recv()
        acc[:, part] += core_rx[:, part]
        axis = first_axis[lane]
        got1.append([
            links.send(
                acc.at[:, at(lane * 512 + lax.rem(at_axis[axis] + d, SIDE) * BLK, BLK)],
                rx1.at[lane, d - 1],
                **step(axis, d),
            )
            for d in (1, 2, 3)
        ])
    get_pl.wait()

    @pl.loop(0, KDIM // 512)
    def _(t):
        cols = at(t * 512, 512)
        g_hi[:COLS, cols], g_lo[:COLS, cols] = split(mm(ot[:COLS, :], plv[:, cols]))

    got2 = []
    for lane in range(LANES):
        axis = second_axis[lane]
        arrived(got1[lane])
        mine = acc[:, at(lane * 512 + at_axis[first_axis[lane]] * BLK, BLK)]
        s1[lane] = (mine + rx1[lane, 0]) + (rx1[lane, 1] + rx1[lane, 2])
        got2.append([
            links.send(
                s1.at[lane, at(lax.rem(at_axis[axis] + d, SIDE) * 64, 64), :],
                rx2.at[lane, d - 1],
                **step(axis, d),
            )
            for d in (1, 2, 3)
        ])

    def summed(q, crx, part_acc, rx_a, sum_a, rx_b, z_b, res, both):
        mine_cols, other_cols = at(core * BLK, BLK), at(other * BLK, BLK)
        copy = links.send(q.at[:, other_cols], crx, core=other)
        yield
        copy.wait_recv()
        part_acc[...] = q[:, mine_cols] + crx[...]
        got = []
        for lane in range(LANES):
            axis = first_axis[lane]
            got.append([
                links.send(
                    part_acc.at[at(lane * 256 + lax.rem(at_axis[axis] + d, SIDE) * 64, 64), :],
                    rx_a.at[lane, d - 1],
                    **step(axis, d),
                )
                for d in (1, 2, 3)
            ])
        yield
        got_b = []
        for lane in range(LANES):
            arrived(got[lane])
            mine = part_acc[at(lane * 256 + at_axis[first_axis[lane]] * 64, 64), :]
            sum_a[lane] = (mine + rx_a[lane, 0]) + (rx_a[lane, 1] + rx_a[lane, 2])
            axis = second_axis[lane]
            got_b.append([
                links.send(
                    sum_a.at[lane, at(lax.rem(at_axis[axis] + d, SIDE) * 16, 16), :],
                    rx_b.at[lane, d - 1],
                    **step(axis, d),
                )
                for d in (1, 2, 3)
            ])
        yield
        got_z = []
        for lane in range(LANES):
            arrived(got_b[lane])
            mine = sum_a[lane, at(at_axis[second_axis[lane]] * 16, 16), :]
            slot = z if both and lane else zh
            z_b[lane, slot] = (mine + rx_b[lane, 0]) + (rx_b[lane, 1] + rx_b[lane, 2])
            if both and lane:
                places = [along_z(d) for d in range(1, ZALL)]
            else:
                places = [step("zh", d) for d in (1, 2, 3)]
            got_z.append([links.send(z_b.at[lane, slot], z_b.at[lane, slot], **where) for where in places])
        yield
        got_g = []
        for lane in range(LANES):
            arrived(got_z[lane])
            rows = at(lane * 256 + at_axis[first_axis[lane]] * 64 + at_axis[second_axis[lane]] * 16, 16)
            total = (z_b[lane, 0] + z_b[lane, 1]) + (z_b[lane, 2] + z_b[lane, 3])
            if both and lane:
                total = total + ((z_b[lane, 4] + z_b[lane, 5]) + (z_b[lane, 6] + z_b[lane, 7]))
            res[rows, mine_cols] = total
            block = res.at[rows, mine_cols]
            got_g.append([links.send(block, block, **step(second_axis[lane], d)) for d in (1, 2, 3)])
        yield
        got_h = []
        for lane in range(LANES):
            arrived(got_g[lane])
            block = res.at[at(lane * 256 + at_axis[first_axis[lane]] * 64, 64), mine_cols]
            got_h.append([links.send(block, block, **step(first_axis[lane], d)) for d in (1, 2, 3)])
        yield
        for lane in range(LANES):
            arrived(got_h[lane])
        block = res.at[:, mine_cols]
        copy = links.send(block, block, core=other)
        yield
        copy.wait_recv()
        yield

    swap_half.wait_recv()
    turn_half(zl)
    s_q[:COLS, :] = mm(ot[:COLS, :], o_m[own, :])
    half = pl.ds(pl.multiple_of(HALO + zl * 1024, TILE), 1024)
    ones = jnp.where(zl == 0, o_o[half, :], o_m[half, :])
    s_q[COLS:, :] = mm(ot[at(zl * COLS, COLS), at(zl * 1024, 1024)], ones)
    s_sum = summed(s_q, s_crx, s_acc, s_rx1, s_s1, s_rx2, s_z, s_res, True)
    next(s_sum)

    got3 = []
    for lane in range(LANES):
        arrived(got2[lane])
        mine = s1[lane, at(at_axis[second_axis[lane]] * 64, 64), :]
        s2[lane] = (mine + rx2[lane, 0]) + (rx2[lane, 1] + rx2[lane, 2])
        got3.append([
            links.send(
                s2.at[lane, at(lax.rem(zh + d, ZHI) * 16, 16), :],
                rx3.at[lane, d - 1],
                **step("zh", d),
            )
            for d in (1, 2, 3)
        ])
    next(s_sum)
    half_a, half_b = at(zl * 1024, 1024), at((1 - zl) * 1024, 1024)

    @pl.loop(0, KDIM // 512)
    def _(t):
        cols = at(t * 512, 512)
        g_o[:, cols] = mm(ot[COLS:, half_a], plv[half_a, cols])


    def k_cols(lane):
        return at(core * HALF + lane * 512 + at_axis[first_axis[lane]] * BLK, BLK)

    def c_rows(lane):
        return at(at_axis[second_axis[lane]] * 64, 64)

    got4 = []
    for lane in range(LANES):
        arrived(got3[lane])
        mine = s2[lane, at(zh * 16, 16), :]
        piece = (mine + rx3[lane, 0]) + (rx3[lane, 1] + rx3[lane, 2])
        rows = at(at_axis[second_axis[lane]] * 64 + zh * 16, 16)
        ct[0, rows, k_cols(lane)] = piece.astype(BF16)
        got4.append({
            d: links.send(ct.at[0, rows, k_cols(lane)], ct.at[d % 2, rows, k_cols(lane)], **along_z(d))
            for d in (2, 4, 6, 1, 3, 5, 7)
        })
    next(s_sum)
    get_h.wait()
    arrived(halo)

    @pl.loop(0, ROWS // BLK)
    def _(i):
        rows = at(i * BLK, BLK)
        b_hi[rows, :], b_lo[rows, :] = split(banded(hv[i], near(o_m, i), (off[1, i], off[2, i])))

    got5 = [[], []]

    def gather_second(side):
        for lane in range(LANES):
            arrived([got4[lane][d] for d in range(1, ZALL) if d % 2 == side])
            block = ct.at[side, c_rows(lane), k_cols(lane)]
            got5[side].append([links.send(block, block, **step(second_axis[lane], d)) for d in (1, 2, 3)])

    gather_second(0)
    next(s_sum)
    swap_late = swap(zl * 1024 + EARLY, LATE)
    c_q[:COLS, :] = mm(ot[:COLS, :], b_hi[...]) + mm(ot[:COLS, :], b_lo[...])
    c_q[COLS:, :] = mm(ot[COLS:, half_a], b_hi[half_a, :]) + mm(ot[COLS:, half_a], b_lo[half_a, :])
    got6 = [[], []]

    def gather_first(side):
        for lane in range(LANES):
            arrived(got5[side][lane])
            block = ct.at[side, :, k_cols(lane)]
            got6[side].append([links.send(block, block, **step(first_axis[lane], d)) for d in (1, 2, 3)])

    gather_first(0)
    gather_second(1)

    got7 = [[], []]

    def gather_core(side):
        for lane in range(LANES):
            arrived(got6[side][lane])
            block = ct.at[side, :, at(core * HALF + lane * 512, 512)]
            got7[side].append(links.send(block, block, core=other))

    gather_core(0)
    gather_first(1)
    arrived([swap_early, swap_late])
    turn_half(1 - zl)

    @pl.loop(0, KDIM // 512)
    def _(t):
        cols = at(t * 512, 512)
        g_hi[COLS:, cols], g_lo[COLS:, cols] = split(g_o[:, cols] + mm(ot[COLS:, half_b], plv[half_b, cols]))

    c_q[COLS:, :] += mm(ot[COLS:, half_b], b_hi[half_b, :]) + mm(ot[COLS:, half_b], b_lo[half_b, :])

    def with_coupling(k):
        c_q[...] += mm_nt(g_hi[:, k], ct[0, :, k]) + mm_nt(g_lo[:, k], ct[0, :, k])

    with_coupling(at(core * HALF, HALF))
    arrived(got7[0])
    with_coupling(at(other * HALF, HALF))
    c_sum = summed(c_q, c_crx, c_acc, c_rx1, c_s1, c_rx2, c_z, c_res, False)
    next(c_sum)
    halo_o = [
        links.send(o_o.at[last, :], o_o.at[before, :], **on_wire(1)),
        links.send(o_o.at[first, :], o_o.at[after, :], **on_wire(-1)),
    ]
    put_o = load(o_o.at[own, :], cols_o, 7)
    gather_core(1)
    next(s_sum)
    next(c_sum)
    next(s_sum)
    next(c_sum)
    next(s_sum)
    next(c_sum)
    next(s_sum)

    scale = 1.0 / TOTAL
    row = lax.broadcasted_iota(jnp.int32, (COLS, COLS), 0)
    col = lax.broadcasted_iota(jnp.int32, (COLS, COLS), 1)
    m_m = jnp.where(row == col, 2.0, 0.0) - s_res[:COLS, :] * scale
    s_01 = 0.0 - s_res[COLS:, :] * scale
    s_10 = s_01.T
    m_o = jnp.where(zl == 1, s_01, s_10)
    m2[0, :, :COLS], m2[0, :, COLS:] = split(m_m)
    m2[1, :, :COLS], m2[1, :, COLS:] = split(m_o)
    mt[:COLS, :COLS], mt[COLS:, :COLS] = split(m_m.T)
    mt[:COLS, COLS:], mt[COLS:, COLS:] = split(jnp.where(zl == 1, s_10, s_01))
    arrived(got7[1])

    @pl.loop(0, KDIM // 512)
    def _(t):
        cols = at(t * 512, 512)
        both = mm(mt[:, :COLS], ct[0, :, cols]) + mm(mt[:, COLS:], ct[1, :, cols])
        d2[:COLS, cols], d2[COLS:, cols] = split(both[:COLS, :] + both[COLS:, :])

    arrived(halo_o)

    @pl.loop(0, (ROWS + 2 * HALO) // 512)
    def _(t):
        rows = at(t * 512, 512)
        both = mm(o_m[rows, :], m2[0]) + mm(o_o[rows, :], m2[1])
        y2[rows, :COLS], y2[rows, COLS:] = split(both[:, :COLS] + both[:, COLS:])

    next(c_sum)
    @pl.loop(0, ROWS // BLK)
    def _(i):
        both = banded(hv[i], near(y2, i), (off[1, i], off[2, i]))
        rest[at(i * BLK, BLK), :] = both[:, :COLS] + both[:, COLS:]


    def with_left(t):
        rows = pl.ds(t * 1024, 1024)
        both = mm_nt(plv[rows, :], d2[...])
        rest[rows, :] += both[:, :COLS] + both[:, COLS:]

    next(c_sum)
    with_left(0)
    with_left(1)
    put_base = load(rest, base, 8)
    next(c_sum)
    next(c_sum)
    put_cross = load(c_res, cross, 9)
    for copy in (put_o, put_base, put_cross):
        copy.wait()
    links.finish()


def last_kernel(base, o_m, o_o, cross, out, x2):
    @pl.when(pl.program_id(0) == 0)
    def _():
        x2[:, :COLS], x2[:, COLS:] = split(cross[...] * (1.0 / TOTAL))

    both = mm(o_m[...], x2[:COLS, :]) + mm(o_o[...], x2[COLS:, :])
    out[...] = base[...] - (both[:, :COLS] + both[:, COLS:])


def body(hamiltonian, offsets, phase_left, phase_right, orbitals):
    def sums(depth):
        return [
            pltpu.VMEM((512, 256), F32),
            pltpu.VMEM((512, 128), F32),
            pltpu.VMEM((512, 128), F32),
            pltpu.VMEM((2, 3, 64, 128), F32),
            pltpu.VMEM((2, 64, 128), F32),
            pltpu.VMEM((2, 3, 16, 128), F32),
            pltpu.VMEM((2, depth, 16, 128), F32),
            pltpu.VMEM((512, 256), F32),
        ]

    hbm = pl.BlockSpec(memory_space=pl.ANY)
    base, cols_o, cross = pl.pallas_call(
        kernel,
        out_shape=[
            jax.ShapeDtypeStruct((ROWS, COLS), F32),
            jax.ShapeDtypeStruct((ROWS, COLS), BF16),
            jax.ShapeDtypeStruct((2 * COLS, COLS), F32),
        ],
        in_specs=[hbm, pl.BlockSpec(memory_space=pltpu.SMEM), hbm, hbm, hbm],
        out_specs=[hbm, hbm, hbm],
        scratch_shapes=[
            pltpu.VMEM((ROWS + 2 * HALO, COLS), BF16),
            pltpu.VMEM((ROWS + 2 * HALO, COLS), BF16),
            pltpu.VMEM((2 * COLS, ROWS), BF16),
            pltpu.VMEM((ROWS, KDIM), BF16),
            pltpu.VMEM((ROWS, KDIM), BF16),
            pltpu.VMEM((16, 3, BLK, BLK), BF16),
            pltpu.VMEM((COLS, HALF), F32),
            pltpu.VMEM((COLS, HALF), F32),
            pltpu.VMEM((COLS, HALF), F32),
            pltpu.VMEM((2, 3, 256, 128), F32),
            pltpu.VMEM((2, 256, 128), F32),
            pltpu.VMEM((2, 3, 64, 128), F32),
            pltpu.VMEM((2, 64, 128), F32),
            pltpu.VMEM((2, 3, 16, 128), F32),
            pltpu.VMEM((2, COLS, KDIM), BF16),
            pltpu.VMEM((ROWS, COLS), BF16),
            pltpu.VMEM((ROWS, COLS), BF16),
            pltpu.VMEM((COLS, KDIM), F32),
            pltpu.VMEM((2 * COLS, KDIM), BF16),
            pltpu.VMEM((2 * COLS, KDIM), BF16),
            *sums(ZALL),
            *sums(ZHI),
            pltpu.VMEM((2 * COLS, 2 * COLS), BF16),
            pltpu.VMEM((2, COLS, 2 * COLS), BF16),
            pltpu.VMEM((2 * COLS, KDIM), BF16),
            pltpu.VMEM((ROWS + 2 * HALO, 2 * COLS), BF16),
            pltpu.VMEM((ROWS, COLS), F32),
            pltpu.SemaphoreType.DMA((10,)),
            pltpu.SemaphoreType.DMA((N_SEMS,)),
            pltpu.SemaphoreType.DMA((N_SEMS,)),
        ],
        compiler_params=pltpu.CompilerParams(
            collective_id=0, has_side_effects=True, vmem_limit_bytes=58 << 20
        ),
        cost_estimate=pl.CostEstimate(flops=16 * 10**9, bytes_accessed=20 * 2**20, transcendentals=0),
    )(hamiltonian, offsets.T, phase_left, phase_right, orbitals)
    tile = pl.BlockSpec((1024, COLS), lambda i: (i, 0))
    whole = pl.BlockSpec((2 * COLS, COLS), lambda i: (0, 0))
    return pl.pallas_call(
        last_kernel,
        grid=(ROWS // 1024,),
        out_shape=jax.ShapeDtypeStruct((ROWS, COLS), F32),
        in_specs=[tile, tile, tile, whole],
        out_specs=tile,
        scratch_shapes=[pltpu.VMEM((2 * COLS, 2 * COLS), BF16)],
        compiler_params=pltpu.CompilerParams(vmem_limit_bytes=60 << 20),
    )(base, orbitals, cols_o, cross)


def solution(mesh):
    finer = Mesh(mesh.devices.reshape(SIDE, ZHI, SIDE, 2, mesh.shape["col"]), AXES)
    in_specs = (
        P(WIRE, None, None, None),
        P(WIRE, None),
        P(WIRE, None),
        P(WIRE, None),
        P(WIRE, "zl"),
    )
    return jax.shard_map(body, mesh=finer, in_specs=in_specs, out_specs=P(WIRE, "zl"), check_vma=False)
```

```python
import jax
import jax.numpy as jnp
from jax import lax
from jax.experimental import pallas as pl
from jax.experimental.pallas import tpu as pltpu
from jax.sharding import Mesh
from jax.sharding import PartitionSpec as P

F32, BF16 = jnp.float32, jnp.bfloat16
MESH = pl.DeviceIdType.MESH
AXES = ("x", "zh", "y", "core", "zl")
WIRE = ("x", "zh", "y", "core")
SIDE, ZHI, ZALL = 4, 4, 8
LANES = 2
HALO, ROWS, COLS, KDIM, BLK = 256, 2048, 256, 2048, 128
HALF = KDIM // 2
TOTAL = 262144
TILE = 256


def mm(a, b):
    return jnp.dot(a, b, preferred_element_type=F32)


def mm_nt(a, b):
    return lax.dot_general(a, b, (((1,), (1,)), ((), ())), preferred_element_type=F32)


def split(v):
    hi = v.astype(BF16)
    return hi, (v - hi.astype(F32)).astype(BF16)


def at(start, size):
    return pl.ds(pl.multiple_of(start, size), size)


def near(src, i):
    return [src[at((i + r) * BLK, BLK), :] for r in range(5)]


def banded(h, blocks, shifts):
    left = jnp.concatenate([h[0], h[1], h[2]], axis=1)
    right = jnp.concatenate([blocks[2], pick(blocks, shifts[0]), pick(blocks, shifts[1])], axis=0)
    return mm(left, right)


def pick(blocks, shift):
    chosen = blocks[2]
    for r in (0, 1, 3, 4):
        chosen = jnp.where(shift == r - 2, blocks[r], chosen)
    return chosen


class Links:
    def __init__(self, send_sems, recv_sems):
        self.send_sems, self.recv_sems, self.started = send_sems, recv_sems, []

    def send(self, src, dst, **where):
        i = len(self.started)
        copy = pltpu.make_async_remote_copy(
            src_ref=src,
            dst_ref=dst,
            send_sem=self.send_sems.at[i],
            recv_sem=self.recv_sems.at[i],
            device_id=where,
            device_id_type=MESH,
        )
        copy.start()
        self.started.append(copy)
        return copy

    def finish(self):
        for copy in self.started:
            copy.wait_send()


N_SEMS = 140
EARLY, LATE = 256, 768


def kernel(
    ham, off, phase_l, phase_r, orb, base, cols_o, cross,
    o_m, o_o, ot, pr, plv, hv,
    core_tx, core_rx, acc, rx1, s1, rx2, s2, rx3, ct, b_hi, b_lo, g_o, g_hi, g_lo,
    s_q, s_crx, s_acc, s_rx1, s_s1, s_rx2, s_z, s_res,
    c_q, c_crx, c_acc, c_rx1, c_s1, c_rx2, c_z, c_res,
    mt, m2, d2, y2, rest,
    load_sems, send_sems, recv_sems,
):
    at_axis = {a: lax.axis_index(a) for a in AXES}
    core, zl, zh = at_axis["core"], at_axis["zl"], at_axis["zh"]
    other = 1 - core
    z = zh * 2 + zl
    wire = ((at_axis["x"] * ZHI + zh) * SIDE + at_axis["y"]) * 2 + core
    n_wire = SIDE * ZHI * SIDE * 2
    first_axis, second_axis = ("x", "y"), ("y", "x")

    def step(axis, d):
        return {axis: lax.rem(at_axis[axis] + d, SIDE)}

    def along_z(d):
        there = lax.rem(z + d, ZALL)
        return {"zh": there // 2, "zl": lax.rem(there, 2)}

    def on_wire(d):
        w = lax.rem(wire + d + n_wire, n_wire)
        return {
            "x": w // (ZHI * SIDE * 2),
            "zh": lax.rem(w // (SIDE * 2), ZHI),
            "y": lax.rem(w // 2, SIDE),
            "core": lax.rem(w, 2),
        }

    links = Links(send_sems, recv_sems)
    own = pl.ds(HALO, ROWS)

    def arrived(copies):
        for copy in copies:
            copy.wait_recv()

    def load(src, dst, i):
        copy = pltpu.make_async_copy(src, dst, load_sems.at[i])
        copy.start()
        return copy

    get_o = load(orb, o_m.at[own, :], 0)
    get_pr = []
    for i in range(4):
        start = (other if i < 2 else core) * HALF + (i % 2) * 512
        cols = at(start, 512)
        get_pr.append(load(phase_r.at[:, cols], pr.at[:, cols], 1 + i))
    barrier = pltpu.get_barrier_semaphore()
    greeted = [step(a, d) for a in ("x", "y") for d in (1, 2, 3)]
    greeted += [along_z(d) for d in range(1, ZALL)]
    greeted += [{"core": other}, on_wire(1), on_wire(-1)]
    for where in greeted:
        pl.semaphore_signal(barrier, inc=1, device_id=where, device_id_type=MESH)
    get_o.wait()
    pl.semaphore_wait(barrier, len(greeted))

    def swap(start, size):
        part = pl.ds(pl.multiple_of(HALO + start, TILE), size)
        return links.send(o_m.at[part, :], o_o.at[part, :], zl=1 - zl)

    last, first = pl.ds(ROWS, HALO), pl.ds(HALO, HALO)
    before, after = pl.ds(0, HALO), pl.ds(HALO + ROWS, HALO)
    halo = [
        links.send(o_m.at[last, :], o_m.at[before, :], **on_wire(1)),
        links.send(o_m.at[first, :], o_m.at[after, :], **on_wire(-1)),
    ]
    swap_half = swap((1 - zl) * 1024, 1024)
    swap_early = swap(zl * 1024, EARLY)

    @pl.loop(0, ROWS // 512)
    def _(t):
        inner = pl.ds(pl.multiple_of(HALO + t * 512, TILE), 512)
        ot[:COLS, at(t * 512, 512)] = o_m[inner, :].T

    def turn_half(half):
        @pl.loop(0, 2)
        def _(t):
            start = half * 1024 + t * 512
            inner = pl.ds(pl.multiple_of(HALO + start, TILE), 512)
            ot[COLS:, at(start, 512)] = o_o[inner, :].T

    def coupling(dst, j, k_start):
        dst[:, j * 512 : (j + 1) * 512] = mm(ot[:COLS, :], pr[:, at(k_start + j * 512, 512)])

    to_core = []
    for j in range(2):
        get_pr[j].wait()
        coupling(core_tx, j, other * HALF)
        part = pl.ds(j * 512, 512)
        to_core.append(links.send(core_tx.at[:, part], core_rx.at[:, part], core=other))
    for j in range(2):
        get_pr[2 + j].wait()
        coupling(acc, j, core * HALF)
    get_h = load(ham, hv, 5)
    get_pl = load(phase_l, plv, 6)

    got1 = []
    for lane in range(LANES):
        part = pl.ds(lane * 512, 512)
        to_core[lane].wait_recv()
        acc[:, part] += core_rx[:, part]
        axis = first_axis[lane]
        got1.append([
            links.send(
                acc.at[:, at(lane * 512 + lax.rem(at_axis[axis] + d, SIDE) * BLK, BLK)],
                rx1.at[lane, d - 1],
                **step(axis, d),
            )
            for d in (1, 2, 3)
        ])
    get_pl.wait()

    @pl.loop(0, KDIM // 512)
    def _(t):
        cols = at(t * 512, 512)
        g_hi[:COLS, cols], g_lo[:COLS, cols] = split(mm(ot[:COLS, :], plv[:, cols]))

    got2 = []
    for lane in range(LANES):
        axis = second_axis[lane]
        arrived(got1[lane])
        mine = acc[:, at(lane * 512 + at_axis[first_axis[lane]] * BLK, BLK)]
        s1[lane] = (mine + rx1[lane, 0]) + (rx1[lane, 1] + rx1[lane, 2])
        got2.append([
            links.send(
                s1.at[lane, at(lax.rem(at_axis[axis] + d, SIDE) * 64, 64), :],
                rx2.at[lane, d - 1],
                **step(axis, d),
            )
            for d in (1, 2, 3)
        ])

    def summed(q, crx, part_acc, rx_a, sum_a, rx_b, z_b, res, both):
        mine_cols, other_cols = at(core * BLK, BLK), at(other * BLK, BLK)
        copy = links.send(q.at[:, other_cols], crx, core=other)
        yield
        copy.wait_recv()
        part_acc[...] = q[:, mine_cols] + crx[...]
        got = []
        for lane in range(LANES):
            axis = first_axis[lane]
            got.append([
                links.send(
                    part_acc.at[at(lane * 256 + lax.rem(at_axis[axis] + d, SIDE) * 64, 64), :],
                    rx_a.at[lane, d - 1],
                    **step(axis, d),
                )
                for d in (1, 2, 3)
            ])
        yield
        got_b = []
        for lane in range(LANES):
            arrived(got[lane])
            mine = part_acc[at(lane * 256 + at_axis[first_axis[lane]] * 64, 64), :]
            sum_a[lane] = (mine + rx_a[lane, 0]) + (rx_a[lane, 1] + rx_a[lane, 2])
            axis = second_axis[lane]
            got_b.append([
                links.send(
                    sum_a.at[lane, at(lax.rem(at_axis[axis] + d, SIDE) * 16, 16), :],
                    rx_b.at[lane, d - 1],
                    **step(axis, d),
                )
                for d in (1, 2, 3)
            ])
        yield
        got_z = []
        for lane in range(LANES):
            arrived(got_b[lane])
            mine = sum_a[lane, at(at_axis[second_axis[lane]] * 16, 16), :]
            slot = z if both and lane else zh
            z_b[lane, slot] = (mine + rx_b[lane, 0]) + (rx_b[lane, 1] + rx_b[lane, 2])
            if both and lane:
                places = [along_z(d) for d in range(1, ZALL)]
            else:
                places = [step("zh", d) for d in (1, 2, 3)]
            got_z.append([links.send(z_b.at[lane, slot], z_b.at[lane, slot], **where) for where in places])
        yield
        got_g = []
        for lane in range(LANES):
            arrived(got_z[lane])
            rows = at(lane * 256 + at_axis[first_axis[lane]] * 64 + at_axis[second_axis[lane]] * 16, 16)
            total = (z_b[lane, 0] + z_b[lane, 1]) + (z_b[lane, 2] + z_b[lane, 3])
            if both and lane:
                total = total + ((z_b[lane, 4] + z_b[lane, 5]) + (z_b[lane, 6] + z_b[lane, 7]))
            res[rows, mine_cols] = total
            block = res.at[rows, mine_cols]
            got_g.append([links.send(block, block, **step(second_axis[lane], d)) for d in (1, 2, 3)])
        yield
        got_h = []
        for lane in range(LANES):
            arrived(got_g[lane])
            block = res.at[at(lane * 256 + at_axis[first_axis[lane]] * 64, 64), mine_cols]
            got_h.append([links.send(block, block, **step(first_axis[lane], d)) for d in (1, 2, 3)])
        yield
        for lane in range(LANES):
            arrived(got_h[lane])
        block = res.at[:, mine_cols]
        copy = links.send(block, block, core=other)
        yield
        copy.wait_recv()
        yield

    swap_half.wait_recv()
    turn_half(zl)
    s_q[:COLS, :] = mm(ot[:COLS, :], o_m[own, :])
    half = pl.ds(pl.multiple_of(HALO + zl * 1024, TILE), 1024)
    ones = jnp.where(zl == 0, o_o[half, :], o_m[half, :])
    s_q[COLS:, :] = mm(ot[at(zl * COLS, COLS), at(zl * 1024, 1024)], ones)
    s_sum = summed(s_q, s_crx, s_acc, s_rx1, s_s1, s_rx2, s_z, s_res, True)
    next(s_sum)

    got3 = []
    for lane in range(LANES):
        arrived(got2[lane])
        mine = s1[lane, at(at_axis[second_axis[lane]] * 64, 64), :]
        s2[lane] = (mine + rx2[lane, 0]) + (rx2[lane, 1] + rx2[lane, 2])
        got3.append([
            links.send(
                s2.at[lane, at(lax.rem(zh + d, ZHI) * 16, 16), :],
                rx3.at[lane, d - 1],
                **step("zh", d),
            )
            for d in (1, 2, 3)
        ])
    next(s_sum)
    half_a, half_b = at(zl * 1024, 1024), at((1 - zl) * 1024, 1024)

    @pl.loop(0, KDIM // 512)
    def _(t):
        cols = at(t * 512, 512)
        g_o[:, cols] = mm(ot[COLS:, half_a], plv[half_a, cols])


    def k_cols(lane):
        return at(core * HALF + lane * 512 + at_axis[first_axis[lane]] * BLK, BLK)

    def c_rows(lane):
        return at(at_axis[second_axis[lane]] * 64, 64)

    got4 = []
    for lane in range(LANES):
        arrived(got3[lane])
        mine = s2[lane, at(zh * 16, 16), :]
        piece = (mine + rx3[lane, 0]) + (rx3[lane, 1] + rx3[lane, 2])
        rows = at(at_axis[second_axis[lane]] * 64 + zh * 16, 16)
        ct[0, rows, k_cols(lane)] = piece.astype(BF16)
        got4.append({
            d: links.send(ct.at[0, rows, k_cols(lane)], ct.at[d % 2, rows, k_cols(lane)], **along_z(d))
            for d in (2, 4, 6, 1, 3, 5, 7)
        })
    next(s_sum)
    get_h.wait()
    arrived(halo)

    @pl.loop(0, ROWS // BLK)
    def _(i):
        rows = at(i * BLK, BLK)
        b_hi[rows, :], b_lo[rows, :] = split(banded(hv[i], near(o_m, i), (off[1, i], off[2, i])))

    got5 = [[], []]

    def gather_second(side):
        for lane in range(LANES):
            arrived([got4[lane][d] for d in range(1, ZALL) if d % 2 == side])
            block = ct.at[side, c_rows(lane), k_cols(lane)]
            got5[side].append([links.send(block, block, **step(second_axis[lane], d)) for d in (1, 2, 3)])

    gather_second(0)
    next(s_sum)
    swap_late = swap(zl * 1024 + EARLY, LATE)
    c_q[:COLS, :] = mm(ot[:COLS, :], b_hi[...]) + mm(ot[:COLS, :], b_lo[...])
    c_q[COLS:, :] = mm(ot[COLS:, half_a], b_hi[half_a, :]) + mm(ot[COLS:, half_a], b_lo[half_a, :])
    got6 = [[], []]

    def gather_first(side):
        for lane in range(LANES):
            arrived(got5[side][lane])
            block = ct.at[side, :, k_cols(lane)]
            got6[side].append([links.send(block, block, **step(first_axis[lane], d)) for d in (1, 2, 3)])

    gather_first(0)
    gather_second(1)

    got7 = [[], []]

    def gather_core(side):
        for lane in range(LANES):
            arrived(got6[side][lane])
            block = ct.at[side, :, at(core * HALF + lane * 512, 512)]
            got7[side].append(links.send(block, block, core=other))

    gather_core(0)
    gather_first(1)
    def with_coupling(top):
        rows = pl.ds(top, COLS)
        c_q[rows, :] += mm_nt(g_hi[rows, :], ct[0]) + mm_nt(g_lo[rows, :], ct[0])

    arrived(got7[0])
    with_coupling(0)
    arrived([swap_early, swap_late])
    turn_half(1 - zl)

    @pl.loop(0, KDIM // 512)
    def _(t):
        cols = at(t * 512, 512)
        g_hi[COLS:, cols], g_lo[COLS:, cols] = split(g_o[:, cols] + mm(ot[COLS:, half_b], plv[half_b, cols]))

    c_q[COLS:, :] += mm(ot[COLS:, half_b], b_hi[half_b, :]) + mm(ot[COLS:, half_b], b_lo[half_b, :])

    with_coupling(COLS)
    c_sum = summed(c_q, c_crx, c_acc, c_rx1, c_s1, c_rx2, c_z, c_res, False)
    next(c_sum)
    halo_o = [
        links.send(o_o.at[last, :], o_o.at[before, :], **on_wire(1)),
        links.send(o_o.at[first, :], o_o.at[after, :], **on_wire(-1)),
    ]
    put_o = load(o_o.at[own, :], cols_o, 7)
    gather_core(1)
    next(s_sum)
    next(c_sum)
    next(s_sum)
    next(c_sum)
    next(s_sum)
    next(c_sum)
    next(s_sum)

    scale = 1.0 / TOTAL
    row = lax.broadcasted_iota(jnp.int32, (COLS, COLS), 0)
    col = lax.broadcasted_iota(jnp.int32, (COLS, COLS), 1)
    m_m = jnp.where(row == col, 2.0, 0.0) - s_res[:COLS, :] * scale
    s_01 = 0.0 - s_res[COLS:, :] * scale
    s_10 = s_01.T
    m_o = jnp.where(zl == 1, s_01, s_10)
    m2[0, :, :COLS], m2[0, :, COLS:] = split(m_m)
    m2[1, :, :COLS], m2[1, :, COLS:] = split(m_o)
    mt[:COLS, :COLS], mt[COLS:, :COLS] = split(m_m.T)
    mt[:COLS, COLS:], mt[COLS:, COLS:] = split(jnp.where(zl == 1, s_10, s_01))
    arrived(got7[1])

    @pl.loop(0, KDIM // 512)
    def _(t):
        cols = at(t * 512, 512)
        both = mm(mt[:, :COLS], ct[0, :, cols]) + mm(mt[:, COLS:], ct[1, :, cols])
        d2[:COLS, cols], d2[COLS:, cols] = split(both[:COLS, :] + both[COLS:, :])

    arrived(halo_o)

    @pl.loop(0, (ROWS + 2 * HALO) // 512)
    def _(t):
        rows = at(t * 512, 512)
        both = mm(o_m[rows, :], m2[0]) + mm(o_o[rows, :], m2[1])
        y2[rows, :COLS], y2[rows, COLS:] = split(both[:, :COLS] + both[:, COLS:])

    next(c_sum)
    @pl.loop(0, ROWS // BLK)
    def _(i):
        both = banded(hv[i], near(y2, i), (off[1, i], off[2, i]))
        rest[at(i * BLK, BLK), :] = both[:, :COLS] + both[:, COLS:]


    def with_left(t):
        rows = pl.ds(t * 1024, 1024)
        both = mm_nt(plv[rows, :], d2[...])
        rest[rows, :] += both[:, :COLS] + both[:, COLS:]

    next(c_sum)
    with_left(0)
    with_left(1)
    put_base = load(rest, base, 8)
    next(c_sum)
    next(c_sum)
    put_cross = load(c_res, cross, 9)
    for copy in (put_o, put_base, put_cross):
        copy.wait()
    links.finish()


def last_kernel(base, o_m, o_o, cross, out, x2):
    @pl.when(pl.program_id(0) == 0)
    def _():
        x2[:, :COLS], x2[:, COLS:] = split(cross[...] * (1.0 / TOTAL))

    both = mm(o_m[...], x2[:COLS, :]) + mm(o_o[...], x2[COLS:, :])
    out[...] = base[...] - (both[:, :COLS] + both[:, COLS:])


def body(hamiltonian, offsets, phase_left, phase_right, orbitals):
    def sums(depth):
        return [
            pltpu.VMEM((512, 256), F32),
            pltpu.VMEM((512, 128), F32),
            pltpu.VMEM((512, 128), F32),
            pltpu.VMEM((2, 3, 64, 128), F32),
            pltpu.VMEM((2, 64, 128), F32),
            pltpu.VMEM((2, 3, 16, 128), F32),
            pltpu.VMEM((2, depth, 16, 128), F32),
            pltpu.VMEM((512, 256), F32),
        ]

    hbm = pl.BlockSpec(memory_space=pl.ANY)
    base, cols_o, cross = pl.pallas_call(
        kernel,
        out_shape=[
            jax.ShapeDtypeStruct((ROWS, COLS), F32),
            jax.ShapeDtypeStruct((ROWS, COLS), BF16),
            jax.ShapeDtypeStruct((2 * COLS, COLS), F32),
        ],
        in_specs=[hbm, pl.BlockSpec(memory_space=pltpu.SMEM), hbm, hbm, hbm],
        out_specs=[hbm, hbm, hbm],
        scratch_shapes=[
            pltpu.VMEM((ROWS + 2 * HALO, COLS), BF16),
            pltpu.VMEM((ROWS + 2 * HALO, COLS), BF16),
            pltpu.VMEM((2 * COLS, ROWS), BF16),
            pltpu.VMEM((ROWS, KDIM), BF16),
            pltpu.VMEM((ROWS, KDIM), BF16),
            pltpu.VMEM((16, 3, BLK, BLK), BF16),
            pltpu.VMEM((COLS, HALF), F32),
            pltpu.VMEM((COLS, HALF), F32),
            pltpu.VMEM((COLS, HALF), F32),
            pltpu.VMEM((2, 3, 256, 128), F32),
            pltpu.VMEM((2, 256, 128), F32),
            pltpu.VMEM((2, 3, 64, 128), F32),
            pltpu.VMEM((2, 64, 128), F32),
            pltpu.VMEM((2, 3, 16, 128), F32),
            pltpu.VMEM((2, COLS, KDIM), BF16),
            pltpu.VMEM((ROWS, COLS), BF16),
            pltpu.VMEM((ROWS, COLS), BF16),
            pltpu.VMEM((COLS, KDIM), F32),
            pltpu.VMEM((2 * COLS, KDIM), BF16),
            pltpu.VMEM((2 * COLS, KDIM), BF16),
            *sums(ZALL),
            *sums(ZHI),
            pltpu.VMEM((2 * COLS, 2 * COLS), BF16),
            pltpu.VMEM((2, COLS, 2 * COLS), BF16),
            pltpu.VMEM((2 * COLS, KDIM), BF16),
            pltpu.VMEM((ROWS + 2 * HALO, 2 * COLS), BF16),
            pltpu.VMEM((ROWS, COLS), F32),
            pltpu.SemaphoreType.DMA((10,)),
            pltpu.SemaphoreType.DMA((N_SEMS,)),
            pltpu.SemaphoreType.DMA((N_SEMS,)),
        ],
        compiler_params=pltpu.CompilerParams(
            collective_id=0, has_side_effects=True, vmem_limit_bytes=58 << 20
        ),
        cost_estimate=pl.CostEstimate(flops=16 * 10**9, bytes_accessed=20 * 2**20, transcendentals=0),
    )(hamiltonian, offsets.T, phase_left, phase_right, orbitals)
    tile = pl.BlockSpec((1024, COLS), lambda i: (i, 0))
    whole = pl.BlockSpec((2 * COLS, COLS), lambda i: (0, 0))
    return pl.pallas_call(
        last_kernel,
        grid=(ROWS // 1024,),
        out_shape=jax.ShapeDtypeStruct((ROWS, COLS), F32),
        in_specs=[tile, tile, tile, whole],
        out_specs=tile,
        scratch_shapes=[pltpu.VMEM((2 * COLS, 2 * COLS), BF16)],
        compiler_params=pltpu.CompilerParams(vmem_limit_bytes=60 << 20),
    )(base, orbitals, cols_o, cross)


def solution(mesh):
    finer = Mesh(mesh.devices.reshape(SIDE, ZHI, SIDE, 2, mesh.shape["col"]), AXES)
    in_specs = (
        P(WIRE, None, None, None),
        P(WIRE, None),
        P(WIRE, None),
        P(WIRE, None),
        P(WIRE, "zl"),
    )
    return jax.shard_map(body, mesh=finer, in_specs=in_specs, out_specs=P(WIRE, "zl"), check_vma=False)
```
